256 devices in a mesh: seq: 32 (over z, y), dp: 8 (over x, core).
Axes of the slice: x: 4, y: 4, z: 8, core: 2. Of those that a mesh axis runs over, the one named last changes fastest.
Arguments:
- queries: bfloat16 [32768, 32, 128], P(('dp', 'seq')), parts along dimension 0, may hold values from -4.5 to 4.5
- keys: bfloat16 [32768, 32, 128], P(('dp', 'seq')), parts along dimension 0, may hold values from -4.5 to 4.5
- values: bfloat16 [32768, 32, 128], P(('dp', 'seq')), parts along dimension 0, may hold values from -6 to 6
- cotangent: bfloat16 [32768, 32, 128], P(('dp', 'seq')), parts along dimension 0, may hold values from -6 to 6
- clip_ids: int32 [32768], P(('dp', 'seq')), parts along dimension 0, may hold values from 0 to 15, never falling along the last dimension, each value on 1 to 512 neighbouring positions
- clip_step: int32 [128], P('dp'), parts along dimension 0, may hold values from 0 to 999
- clip_weight: float32 [128], P('dp'), parts along dimension 0, may hold values from 0.3 to 3
- step_gate: float32 [1000, 32, 128], P(None, 'seq'), may hold values from -6 to 6
Outputs:
- grad_queries: bfloat16 [32768, 32, 128], P(('dp', 'seq')), parts along dimension 0
- grad_keys: bfloat16 [32768, 32, 128], P(('dp', 'seq')), parts along dimension 0
- grad_values: bfloat16 [32768, 32, 128], P(('dp', 'seq')), parts along dimension 0
- grad_table: float32 [8000, 32, 128], P('dp', 'seq'), parts along dimension 0
The draws below stay inside these ranges and needn't reach their ends.
There are 8 independent parts, one for each index of `dp`. The reference program is written for one: setup_inputs(seed, part) draws one part's arguments, and reference() takes and returns one part's arrays. A program takes and returns all parts, laid end to end along the dimension named above; an argument that names none is the same for every part. Nothing has to cross between parts.
Inputs may be any that keep to these rules, and one draw needn't show every extreme that they name: `clip_ids`: clip numbers never fall along the tokens; each clip holds 1 to 512 tokens, and some clip exactly 512.
All inputs are finite; a program needn't handle non-finite values.
Results may differ from the reference program's by a relative error of at most 0.038.
Values may be sent and summed in bfloat16 or wider, within the bound.
A program may use at most 64 MiB of HBM per device.

```python
import math
import jax
import jax.numpy as jnp
import numpy as np
from jax import lax

HD = 128
HEADS = 32
TOKENS = 4096
MAXCLIP = 512
CLIPS = 16
QBLOCK = 512
NSTEPS = 1000


def draw_queries(key, part):
    key = jax.random.fold_in(key, 11)
    result = jnp.clip(jax.random.normal(key, (TOKENS, HEADS, HD), jnp.float32), -4.5, 4.5)
    return result.astype(jnp.bfloat16)


def draw_keys(key, part):
    key = jax.random.fold_in(key, 23)
    result = jnp.clip(jax.random.normal(key, (TOKENS, HEADS, HD), jnp.float32), -4.5, 4.5)
    return result.astype(jnp.bfloat16)


def place_ends(values, own_key, smallest, largest):
    spot = [jax.random.randint(jax.random.fold_in(own_key, axis), (), 0, length) for axis, length in enumerate(values.shape)]
    longest = values.shape.index(max(values.shape))
    beside = spot[:longest] + [(spot[longest] + 1) % values.shape[longest]] + spot[longest + 1:]
    return values.at[tuple(spot)].set(smallest).at[tuple(beside)].set(largest)


def shard_levels(own_key, dims, cuts, smallest, top_value):
    factor_of, own = 1.0, jax.random.fold_in(own_key, 6)
    for axis_at, blocks in cuts:
        heights = jnp.exp(jax.random.uniform(jax.random.fold_in(own, axis_at), (blocks,), jnp.float32, smallest / len(cuts), top_value / len(cuts)))
        factor_of = factor_of * jnp.repeat(heights, dims[axis_at] // blocks).reshape([-1 if axis == axis_at else 1 for axis in range(len(dims))])
    return factor_of


def split_up(number_of, total, reach, slope):
    loads = [(1 << 20) // math.isqrt(standing ** slope) + 1 for standing in range(2, number_of + 1)]
    spare, holding = total - reach - (number_of - 1), [1] * (number_of - 1)
    while spare > 0:
        movable = [i for i in range(number_of - 1) if holding[i] < reach]
        pool, left = sum([loads[i] for i in movable]), spare
        for i in movable:
            addition = min(reach - holding[i], max(1, left * loads[i] // pool), spare)
            holding[i] = holding[i] + addition
            spare = spare - addition
    return np.array([reach] + holding)


def uneven(stream_key, count, total, most, lean):
    if count == 2:
        one = jax.random.randint(stream_key, (), max(1, total - most), min(most, total - 1) + 1)
        return jnp.stack([one, total - one])
    tallies = jnp.asarray(split_up(count, total, most, lean), jnp.int32)
    couples = (count - 1) // 2
    source_of, taker = tallies[1:1 + 2 * couples:2], tallies[2:2 + 2 * couples:2]
    room = jnp.minimum(source_of - 1, most - taker)
    shifted = jax.random.randint(jax.random.fold_in(stream_key, 1), (couples,), 0, 1 << 20) % (room + 1)
    tallies = tallies.at[1:1 + 2 * couples:2].set(source_of - shifted).at[2:2 + 2 * couples:2].set(taker + shifted)
    return tallies[jax.random.permutation(jax.random.fold_in(stream_key, 2), count)]


def normal_values(own_key, shape, scale, limit, pieces=(), kind=jnp.bfloat16):
    gain = shard_levels(own_key, shape, pieces, -0.22, 0.18) if pieces else 1.0
    entries = jax.random.normal(own_key, shape, jnp.float32) * scale * gain
    return jnp.minimum(jnp.maximum(entries, -limit), limit).astype(kind)


def setup_inputs(seed: int = 0, part: int = 0) -> dict:
    key_of = jax.random.split(jax.random.key(seed), 9)
    own_keys = jax.random.split(jax.random.fold_in(key_of[8], part), 9)
    queries = draw_queries(jax.random.fold_in(jax.random.fold_in(key_of[8], part), 71), part)
    keys = draw_keys(jax.random.fold_in(jax.random.fold_in(key_of[8], part), 71), part)
    values = normal_values(own_keys[2], (TOKENS, HEADS, HD), 1.0, 6.0, ((0, 32),))
    cotangent = normal_values(own_keys[3], (TOKENS, HEADS, HD), 1.0, 6.0, ((0, 32),))
    clip_ids = jnp.searchsorted(jnp.cumsum(uneven(own_keys[4], CLIPS, TOKENS, MAXCLIP, 2)), jnp.arange(TOKENS), side="right").astype(jnp.int32)
    clip_step = place_ends(jax.random.randint(own_keys[5], (CLIPS,), 0, NSTEPS), jax.random.fold_in(own_keys[5], 1), 0, NSTEPS - 1).astype(jnp.int32)
    clip_weight = jnp.clip(jnp.exp(jax.random.uniform(own_keys[6], (CLIPS,), jnp.float32, math.log(0.3), math.log(3.0))), 0.3, 3.0)
    step_gate = normal_values(key_of[7], (NSTEPS, HEADS, HD), 1.0, 6.0, ((1, 32),), jnp.float32)
    return dict(queries=queries, keys=keys, values=values, cotangent=cotangent, clip_ids=clip_ids, clip_step=clip_step, clip_weight=clip_weight, step_gate=step_gate)


def attend_head(head_q, head_k, head_v, head_dout, token_ids):
    total = head_q.shape[0]
    width = min(QBLOCK + 2 * MAXCLIP, total)
    blocks = total // QBLOCK
    factor = 1.0 / math.sqrt(head_q.shape[1])
    zeros_f = jnp.zeros(head_q.shape, jnp.float32)
    zeros_b = jnp.zeros(head_q.shape, jnp.bfloat16)

    def one_block(block, carry):
        acc_keys, acc_values, out_dq, out_attn = carry
        row_start = (block * QBLOCK).astype(jnp.int32)
        ids_rows = lax.dynamic_slice_in_dim(token_ids, row_start, QBLOCK)
        begin = jnp.sum((token_ids < ids_rows[0]).astype(jnp.int32))
        begin = jnp.minimum(begin, total - width).astype(jnp.int32)
        rows_q = lax.dynamic_slice_in_dim(head_q, row_start, QBLOCK)
        rows_do = lax.dynamic_slice_in_dim(head_dout, row_start, QBLOCK)
        win_k = lax.dynamic_slice_in_dim(head_k, begin, width)
        win_v = lax.dynamic_slice_in_dim(head_v, begin, width)
        ids_win = lax.dynamic_slice_in_dim(token_ids, begin, width)
        scores = jnp.dot(rows_q, win_k.T, preferred_element_type=jnp.float32) * factor
        same_clip = ids_rows[:, None] == ids_win[None, :]
        scores = jnp.where(same_clip, scores, -1e+30)
        row_max = lax.optimization_barrier(jnp.max(scores, axis=1, keepdims=True))
        expo_terms = jnp.exp(scores - row_max)
        probs = expo_terms / lax.optimization_barrier(jnp.sum(expo_terms, axis=1, keepdims=True))
        probs_b = probs.astype(jnp.bfloat16)
        attn_rows = jnp.dot(probs_b, win_v, preferred_element_type=jnp.float32).astype(jnp.bfloat16)
        d_probs = jnp.dot(rows_do, win_v.T, preferred_element_type=jnp.float32)
        delta = lax.optimization_barrier(jnp.sum(rows_do.astype(jnp.float32) * attn_rows.astype(jnp.float32), axis=1, keepdims=True))
        d_scores = (probs * (d_probs - delta) * factor).astype(jnp.bfloat16)
        dq_rows = jnp.dot(d_scores, win_k, preferred_element_type=jnp.float32).astype(jnp.bfloat16)
        dk_part = jnp.dot(d_scores.T, rows_q, preferred_element_type=jnp.float32)
        dv_part = jnp.dot(probs_b.T, rows_do, preferred_element_type=jnp.float32)
        acc_keys = lax.dynamic_update_slice_in_dim(acc_keys, lax.dynamic_slice_in_dim(acc_keys, begin, width) + dk_part, begin, 0)
        acc_values = lax.dynamic_update_slice_in_dim(acc_values, lax.dynamic_slice_in_dim(acc_values, begin, width) + dv_part, begin, 0)
        out_dq = lax.dynamic_update_slice_in_dim(out_dq, dq_rows, row_start, 0)
        out_attn = lax.dynamic_update_slice_in_dim(out_attn, attn_rows, row_start, 0)
        return (acc_keys, acc_values, out_dq, out_attn)
    acc_keys, acc_values, out_dq, out_attn = lax.fori_loop(0, blocks, one_block, (zeros_f, zeros_f, zeros_b, zeros_b))
    return (out_dq, acc_keys.astype(jnp.bfloat16), acc_values.astype(jnp.bfloat16), out_attn)

def reference(queries, keys, values, cotangent, clip_ids, clip_step, clip_weight, step_gate):
    highest = lax.Precision.HIGHEST
    onehot_tok = (clip_ids[:, None] == jnp.arange(CLIPS, dtype=jnp.int32)[None, :]).astype(jnp.float32)
    onehot_step = (clip_step[:, None] == jnp.arange(NSTEPS, dtype=jnp.int32)[None, :]).astype(jnp.float32)
    gate_clip = jnp.einsum('cn,nhe->che', onehot_step, step_gate, precision=highest)
    weighted = gate_clip * clip_weight[:, None, None]
    token_scale = jnp.einsum('tc,che->the', onehot_tok, weighted, precision=highest)
    d_out = (token_scale * cotangent.astype(jnp.float32)).astype(jnp.bfloat16)

    def per_head(items):
        return attend_head(items[0], items[1], items[2], items[3], clip_ids)
    stacked = (jnp.moveaxis(queries, 1, 0), jnp.moveaxis(keys, 1, 0), jnp.moveaxis(values, 1, 0), jnp.moveaxis(d_out, 1, 0))
    grad_q, grad_k, grad_v, attn_out = lax.map(per_head, stacked)
    grad_q = jnp.moveaxis(grad_q, 0, 1)
    grad_k = jnp.moveaxis(grad_k, 0, 1)
    grad_v = jnp.moveaxis(grad_v, 0, 1)
    attn_out = jnp.moveaxis(attn_out, 0, 1)
    token_weight = jnp.dot(onehot_tok, clip_weight, precision=highest)
    terms = token_weight[:, None, None] * cotangent.astype(jnp.float32) * attn_out.astype(jnp.float32)
    grad_gate = jnp.einsum('tc,the->che', onehot_tok, terms, precision=highest)
    grad_table = jnp.einsum('cn,che->nhe', onehot_step, grad_gate, precision=highest)
    return (grad_q, grad_k, grad_v, grad_table)
```

```python
import math

import jax
import jax.numpy as jnp
from jax import lax
from jax.experimental import pallas as pl
from jax.experimental.pallas import tpu as pltpu
from jax.sharding import PartitionSpec as P

NY = 4
NZ = 8
BLK = 128
ROW = NY * BLK
WIN = 2 * ROW
HD = 128
HEADS = 32
SLOTS = HEADS // NY
CLIPS = 16
STEPS = 1000
GRP = 16
QB = 256
AHEAD = 3
LAG_COMPUTE = 2
LAG_BACK = 5
MESH = pl.DeviceIdType.MESH
F32 = jnp.float32
BF16 = jnp.bfloat16


def nt(a, b):
    return lax.dot_general(a, b, (((1,), (1,)), ((), ())), preferred_element_type=F32)


def nn(a, b):
    return jnp.dot(a, b, preferred_element_type=F32)


def fill_clip_columns(idbuf, idcol):
    def one(b, _):
        line = idbuf[b, 0:1, :].astype(F32)
        idcol[pl.ds(pl.multiple_of(b * BLK, BLK), BLK), :] = jnp.broadcast_to(line, (BLK, BLK)).T
        return 0

    lax.fori_loop(0, 3 * NY, one, 0)


def attend(i, win, res, gate_in, idbuf, idcol, kt, vt, dout, acc):
    parity = lax.rem(i, 2)
    base = NY * (1 - parity)
    kt[...] = win[i, 1].T
    vt[...] = win[i, 2].T
    gate = gate_in[i]
    hi = gate.astype(BF16)
    rest = gate - hi.astype(F32)
    mid = rest.astype(BF16)
    low = (rest - mid.astype(F32)).astype(BF16)
    parts = jnp.concatenate([hi, mid, low, jnp.zeros((HD - 3 * CLIPS, HD), BF16)], axis=0)
    start = pl.multiple_of(base * BLK, BLK)
    lane = (lax.broadcasted_iota(jnp.int32, (WIN, HD), 1) % CLIPS).astype(F32)
    onehot = (idcol[pl.ds(start, WIN), :] == lane).astype(F32).astype(BF16)
    dout[...] = (nn(onehot, parts) * win[i, 3].astype(F32)).astype(BF16)
    acc[...] = jnp.zeros_like(acc)

    factor = 1.0 / math.sqrt(HD)
    not_mine = idcol[pl.ds(2 * ROW - ROW * (1 - parity) - (1 - parity), 1), :]
    edge = idcol[pl.ds(2 * ROW - ROW * parity - (1 - parity), 1), :]
    cid = lax.broadcasted_iota(jnp.int32, (CLIPS, QB), 0).astype(F32)
    per = QB // BLK

    def one(j, sums):
        at = pl.multiple_of(j * QB, QB)
        qb = win[i, 0, pl.ds(at, QB), :]
        db = dout[pl.ds(at, QB), :]
        ids_q = jnp.concatenate([idbuf[base + j * per + u, 0:1, :] for u in range(per)], axis=1)
        ids_q = ids_q.astype(F32)
        ids_k = idcol[pl.ds(start, WIN), :]
        same = jnp.concatenate([ids_k] * per, axis=1) == ids_q
        s = nt(win[i, 1], qb)
        s = jnp.where(same, s * (factor * math.log2(math.e)), -1e30)
        top = jnp.max(s, axis=0, keepdims=True)
        e = jnp.exp2(s - top)
        p = e * (1.0 / jnp.sum(e, axis=0, keepdims=True))
        pb = p.astype(BF16)
        o = nn(vt[...], pb).T.astype(BF16).astype(F32)
        dp = nt(win[i, 2], db)
        delta = jnp.sum((db.astype(F32) * o).T, axis=0, keepdims=True)
        ds = (p * (dp - delta) * factor).astype(BF16)
        res[i, 0, pl.ds(at, QB), :] = nn(kt[...], ds).T.astype(BF16)
        acc[0] += nn(ds, qb)
        acc[1] += nn(pb, db)
        nm = jnp.concatenate([not_mine] * per, axis=1)
        ed = jnp.concatenate([edge] * per, axis=1)
        halo = (j // (ROW // QB) + parity) % 2
        inside = jnp.full((1, QB), 1 - halo, jnp.int32).astype(F32)
        good = jnp.where(ids_q != nm, jnp.where(ids_q == ed, 1.0, inside), 0.0)
        pick = jnp.where(cid == ids_q, good, 0.0).astype(BF16)
        prod = win[i, 3, pl.ds(at, QB), :].astype(F32) * o
        ph = prod.astype(BF16)
        return sums + (nn(pick, ph) + nn(pick, (prod - ph.astype(F32)).astype(BF16)))

    sums = lax.fori_loop(0, WIN // QB, one, jnp.zeros((CLIPS, HD), F32))
    res[i, 1] = acc[0].astype(BF16)
    res[i, 2] = acc[1].astype(BF16)
    return sums


def kernel(
    step_ref, weight_ref, q_hbm, k_hbm, v_hbm, c_hbm, ids_ref, gate_ref,
    dq_ref, dk_ref, dv_ref, table_ref,
    stage, src, win, res, back, fin, idbuf, idcol, kt, vt, dout, acc, gate_in, sum_in, sum_out, wcol,
    perm, load_sem, own_sem,
    yin_s, yin_r, zin_s, zin_r, zout_s, zout_r, yout_s, yout_r, id_s, id_r, gate_s, gate_r, sum_s, sum_r,
):
    me = lax.axis_index("seq")
    z, y = me // NY, lax.rem(me, NY)

    def ypeer(d):
        return {"seq": z * NY + lax.rem(y + d, NY)}

    def zpeer(d):
        return {"seq": lax.rem(z + d, NZ) * NY + y}

    loads = [
        pltpu.make_async_copy(r, stage.at[a], load_sem.at[a])
        for a, r in enumerate((q_hbm, k_hbm, v_hbm, c_hbm))
    ]
    for c in loads:
        c.start()

    barrier = pltpu.get_barrier_semaphore()
    for d in range(1, NY):
        pl.semaphore_signal(barrier, inc=1, device_id=ypeer(d), device_id_type=MESH)
    for d in range(1, NZ):
        pl.semaphore_signal(barrier, inc=1, device_id=zpeer(d), device_id_type=MESH)

    row = lax.broadcasted_iota(jnp.int32, (GRP * GRP, GRP * GRP), 0)
    col = lax.broadcasted_iota(jnp.int32, (GRP * GRP, GRP * GRP), 1)
    perm[...] = (col == (row % GRP) * GRP + row // GRP).astype(F32).astype(BF16)
    for c in range(CLIPS):
        wcol[c : c + 1, :] = jnp.full((1, HD), weight_ref[c], F32)
        gate_in[z, c : c + 1, :] = gate_ref[pl.ds(step_ref[c], 1), :] * weight_ref[c]
    idbuf[NY + y] = jnp.broadcast_to(ids_ref[...], (8, BLK))
    for c in loads:
        c.wait()

    def lay_in(g):
        def one(n, _):
            a, t = n // (BLK // GRP), lax.rem(n, BLK // GRP)
            at = pl.ds(pl.multiple_of(t * GRP, GRP), GRP)
            x = stage[a, at, g * GRP : (g + 1) * GRP, :].reshape(GRP * GRP, HD)
            src[g * GRP : (g + 1) * GRP, a, at, :] = nn(perm[...], x).astype(BF16).reshape(GRP, GRP, HD)
            return 0

        lax.fori_loop(0, 4 * (BLK // GRP), one, 0)

    def lay_out(g):
        def one(t, _):
            at = pl.ds(pl.multiple_of(t * GRP, GRP), GRP)
            for a, out in enumerate((dq_ref, dk_ref, dv_ref)):
                x = fin[g * GRP : (g + 1) * GRP, a, at, :].reshape(GRP * GRP, HD)
                out[at, g * GRP : (g + 1) * GRP, :] = nn(perm[...], x).astype(BF16).reshape(GRP, GRP, HD)
            return 0

        lax.fori_loop(0, BLK // GRP, one, 0)

    def remote(s, d, ss, rs, to):
        return pltpu.make_async_remote_copy(
            src_ref=s, dst_ref=d, send_sem=ss, recv_sem=rs, device_id=to, device_id_type=MESH
        )

    def own_at(i):
        return pl.multiple_of(ROW * lax.rem(i, 2), ROW)

    def yin(i, d):
        to = ypeer(d)
        return remote(
            src.at[NY * i + lax.rem(y + d, NY)],
            win.at[i, :, pl.ds(pl.multiple_of(own_at(i) + y * BLK, BLK), BLK), :],
            yin_s.at[i, d - 1], yin_r.at[i, d - 1], to,
        )

    def own_copy(i):
        return pltpu.make_async_copy(
            src.at[NY * i + y],
            win.at[i, :, pl.ds(pl.multiple_of(own_at(i) + y * BLK, BLK), BLK), :],
            own_sem.at[i],
        )

    def zin(i):
        at = pl.ds(own_at(i), ROW)
        return remote(
            win.at[i, :, at, :], win.at[i, :, pl.ds(pl.multiple_of(ROW - own_at(i), ROW), ROW), :],
            zin_s.at[i], zin_r.at[i], zpeer(jnp.where(lax.rem(i, 2) == 0, NZ - 1, 1)),
        )

    def zout(i):
        at = pl.ds(pl.multiple_of(ROW - own_at(i), ROW), ROW)
        return remote(
            res.at[i, :, at, :], back.at[i],
            zout_s.at[i], zout_r.at[i], zpeer(jnp.where(lax.rem(i, 2) == 0, 1, NZ - 1)),
        )

    def yout(i, d):
        to = lax.rem(y + d, NY)
        return remote(
            res.at[i, :, pl.ds(pl.multiple_of(own_at(i) + to * BLK, BLK), BLK), :],
            fin.at[NY * i + y],
            yout_s.at[i, d - 1], yout_r.at[i, d - 1], ypeer(d),
        )

    def id_y(d):
        return remote(idbuf.at[NY + y], idbuf.at[NY + y], id_s.at[d - 1], id_r.at[d - 1], ypeer(d))

    def id_z(n):
        at = 0 if n == 0 else 2 * NY
        return remote(
            idbuf.at[pl.ds(NY, NY)], idbuf.at[pl.ds(at, NY)],
            id_s.at[NY - 1 + n], id_r.at[NY - 1 + n], zpeer(1 if n == 0 else NZ - 1),
        )

    def gate_copy(d):
        return remote(gate_in.at[z], gate_in.at[z], gate_s.at[d - 1], gate_r.at[d - 1], zpeer(d))

    def sum_copy(i):
        d = lax.rem(i - z + NZ, NZ)
        return remote(sum_out.at[i], sum_in.at[z], sum_s.at[i], sum_r.at[z], zpeer(d))

    lay_in(0)
    pl.semaphore_wait(barrier, NY - 1 + NZ - 1)

    for d in range(1, NY):
        id_y(d).start()
    for d in range(1, NZ):
        gate_copy(d).start()

    def begin(i):
        own_copy(i).start()
        for d in range(1, NY):
            yin(i, d).start()

    for i in range(AHEAD):
        begin(jnp.int32(i))
    lay_in(1)
    for d in range(1, NY):
        id_y(d).wait_recv()
    for n in range(2):
        id_z(n).start()
    for n in range(2):
        id_z(n).wait_recv()
    fill_clip_columns(idbuf, idcol)
    for d in range(1, NZ):
        gate_copy(d).wait_recv()

    def step(t, _):
        @pl.when(t < SLOTS)
        def _():
            own_copy(t).wait()
            for d in range(1, NY):
                yin(t, d).wait_recv()
            zin(t).start()

            @pl.when(t + AHEAD < SLOTS)
            def _():
                begin(t + AHEAD)

        @pl.when((t >= LAG_COMPUTE) & (t < SLOTS + LAG_COMPUTE))
        def _():
            i = t - LAG_COMPUTE
            zin(i).wait_recv()
            sums = attend(i, win, res, gate_in, idbuf, idcol, kt, vt, dout, acc)
            zout(i).start()
            sum_out[i] = sums * wcol[...]

            @pl.when(i != z)
            def _():
                sum_copy(i).start()

            @pl.when(i == z)
            def _():
                sum_in[z] = sum_out[i]

        @pl.when(t >= LAG_BACK)
        def _():
            i = t - LAG_BACK
            zout(i).wait_recv()
            parity = lax.rem(i, 2)
            other = idcol[pl.ds(2 * ROW - ROW * (1 - parity) - (1 - parity), 1), :]
            theirs = idcol[ROW : 2 * ROW, :] == other
            at = pl.ds(own_at(i), ROW)
            for a in range(3):
                res[i, a, at, :] = jnp.where(
                    theirs, back[i, a].astype(F32), res[i, a, at, :].astype(F32)
                ).astype(BF16)
            for d in range(1, NY):
                yout(i, d).start()
            fin[NY * i + y] = res[i, :, pl.ds(pl.multiple_of(own_at(i) + y * BLK, BLK), BLK), :]

        return 0

    lax.fori_loop(0, SLOTS + LAG_BACK, step, 0)

    def arrived(i, _):
        for d in range(1, NY):
            yout(i, d).wait_recv()
        return 0

    lax.fori_loop(0, SLOTS // 2, arrived, 0)
    lay_out(0)

    def sums_arrived(i, _):
        @pl.when(i != z)
        def _():
            remote(
                sum_out.at[i], sum_in.at[i], sum_s.at[i], sum_r.at[i], zpeer(lax.rem(i - z + NZ, NZ))
            ).wait_recv()

        return 0

    lax.fori_loop(0, NZ, sums_arrived, 0)
    total = sum_in[0]
    for r in range(1, NZ):
        total = total + sum_in[r]
    line = lax.broadcasted_iota(jnp.int32, (STEPS, HD), 0)
    table = jnp.zeros((STEPS, HD), F32)
    for c in range(CLIPS):
        table = table + jnp.where(line == step_ref[c], total[c : c + 1, :], 0.0)
    table_ref[...] = table

    lax.fori_loop(SLOTS // 2, SLOTS, arrived, 0)
    lay_out(1)

    def sent(i, _):
        for d in range(1, NY):
            yin(i, d).wait_send()
            yout(i, d).wait_send()
        zin(i).wait_send()
        zout(i).wait_send()

        @pl.when(i != z)
        def _():
            sum_copy(i).wait_send()

        return 0

    lax.fori_loop(0, SLOTS, sent, 0)
    for d in range(1, NY):
        id_y(d).wait_send()
    for n in range(2):
        id_z(n).wait_send()
    for d in range(1, NZ):
        gate_copy(d).wait_send()


def on_device(queries, keys, values, cotangent, clip_ids, clip_step, clip_weight, step_gate):
    vm = pl.BlockSpec(memory_space=pltpu.VMEM)
    sm = pl.BlockSpec(memory_space=pltpu.SMEM)
    hb = pl.BlockSpec(memory_space=pl.ANY)
    dma = pltpu.SemaphoreType.DMA
    grads = jax.ShapeDtypeStruct((BLK, HEADS, HD), BF16)
    dq, dk, dv, table = pl.pallas_call(
        kernel,
        out_shape=(grads, grads, grads, jax.ShapeDtypeStruct((STEPS, HD), F32)),
        in_specs=[sm, sm, hb, hb, hb, hb, vm, vm],
        out_specs=(vm, vm, vm, vm),
        scratch_shapes=[
            pltpu.VMEM((4, BLK, HEADS, HD), BF16),
            pltpu.VMEM((HEADS, 4, BLK, HD), BF16),
            pltpu.VMEM((SLOTS, 4, WIN, HD), BF16),
            pltpu.VMEM((SLOTS, 3, WIN, HD), BF16),
            pltpu.VMEM((SLOTS, 3, ROW, HD), BF16),
            pltpu.VMEM((HEADS, 3, BLK, HD), BF16),
            pltpu.VMEM((3 * NY, 8, BLK), jnp.int32),
            pltpu.VMEM((3 * ROW, BLK), F32),
            pltpu.VMEM((HD, WIN), BF16),
            pltpu.VMEM((HD, WIN), BF16),
            pltpu.VMEM((WIN, HD), BF16),
            pltpu.VMEM((2, WIN, HD), F32),
            pltpu.VMEM((NZ, CLIPS, HD), F32),
            pltpu.VMEM((NZ, CLIPS, HD), F32),
            pltpu.VMEM((NZ, CLIPS, HD), F32),
            pltpu.VMEM((CLIPS, HD), F32),
            pltpu.VMEM((GRP * GRP, GRP * GRP), BF16),
            dma((4,)), dma((SLOTS,)),
            dma((SLOTS, NY - 1)), dma((SLOTS, NY - 1)),
            dma((SLOTS,)), dma((SLOTS,)),
            dma((SLOTS,)), dma((SLOTS,)),
            dma((SLOTS, NY - 1)), dma((SLOTS, NY - 1)),
            dma((NY + 1,)), dma((NY + 1,)),
            dma((NZ - 1,)), dma((NZ - 1,)),
            dma((NZ,)), dma((NZ,)),
        ],
        compiler_params=pltpu.CompilerParams(
            collective_id=0, has_side_effects=True, vmem_limit_bytes=60 * 2**20
        ),
        cost_estimate=pl.CostEstimate(flops=12 * 2**30, bytes_accessed=8 * 2**20, transcendentals=2**23),
        name="clip_attention_backward",
    )(
        clip_step, clip_weight, queries, keys, values, cotangent,
        clip_ids.reshape(1, BLK), step_gate.reshape(STEPS, HD),
    )
    return dq, dk, dv, table.reshape(STEPS, 1, HD)


def solution(mesh):
    in_specs = (
        P(("dp", "seq"), None, None),
        P(("dp", "seq"), None, None),
        P(("dp", "seq"), None, None),
        P(("dp", "seq"), None, None),
        P(("dp", "seq")),
        P("dp"),
        P("dp"),
        P(None, "seq", None),
    )
    out_specs = (
        P(("dp", "seq"), None, None),
        P(("dp", "seq"), None, None),
        P(("dp", "seq"), None, None),
        P("dp", "seq", None),
    )
    return jax.shard_map(
        on_device, mesh=mesh, in_specs=in_specs, out_specs=out_specs, check_vma=False
    )
```

```python
import math

import jax
import jax.numpy as jnp
from jax import lax
from jax.experimental import pallas as pl
from jax.experimental.pallas import tpu as pltpu
from jax.sharding import PartitionSpec as P

NY = 4
NZ = 8
BLK = 128
ROW = NY * BLK
WIN = 2 * ROW
HD = 128
HEADS = 32
SLOTS = HEADS // NY
CLIPS = 16
STEPS = 1000
QB = 256
NEAR = 80.0
AHEAD = 3
LAG_COMPUTE = 3
LAG_BACK = 7
MESH = pl.DeviceIdType.MESH
F32 = jnp.float32
BF16 = jnp.bfloat16


def nt(a, b):
    return lax.dot_general(a, b, (((1,), (1,)), ((), ())), preferred_element_type=F32)


def nn(a, b):
    return jnp.dot(a, b, preferred_element_type=F32)


def fill_clips(idbuf, idcol, hot, near):
    lane = lax.broadcasted_iota(jnp.int32, (BLK, HD), 1)
    clip = (lane % CLIPS).astype(F32)
    once = jnp.where(lane < CLIPS, NEAR, 0.0)

    def one(b, _):
        at = pl.ds(pl.multiple_of(b * BLK, BLK), BLK)
        ids = jnp.broadcast_to(idbuf[b, 0:1, :].astype(F32), (BLK, BLK)).T
        idcol[at, :] = ids
        hot[at, :] = jnp.where(ids == clip, 1.0, 0.0).astype(BF16)
        near[at, :] = jnp.where(ids == clip, once, 0.0).astype(BF16)
        return 0

    lax.fori_loop(0, 3 * NY, one, 0)


def three_parts(x):
    hi = x.astype(BF16)
    rest = x - hi.astype(F32)
    mid = rest.astype(BF16)
    low = (rest - mid.astype(F32)).astype(BF16)
    return jnp.concatenate([hi, mid, low, jnp.zeros((HD - 3 * CLIPS, HD), BF16)], axis=0)


def other_clip(idcol, parity):
    return idcol[pl.ds(2 * ROW - (ROW + 1) * (1 - parity), 1), :]


def attend(i, win, res, gate_in, idbuf, idcol, hot, near, kt, vt, dout, probs, dscores):
    parity = lax.rem(i, 2)
    base = NY * (1 - parity)
    start = pl.multiple_of(base * BLK, BLK)
    kt[...] = win[i, 1].T
    vt[...] = win[i, 2].T
    scale = nn(hot[pl.ds(start, WIN), :], three_parts(gate_in[i]))
    dout[...] = (scale * win[i, 3].astype(F32)).astype(BF16)

    factor = 1.0 / math.sqrt(HD)
    per = QB // BLK
    not_mine = jnp.concatenate([other_clip(idcol, parity)] * per, axis=1)
    edge = jnp.concatenate([idcol[pl.ds(2 * ROW - ROW * parity - (1 - parity), 1), :]] * per, axis=1)
    cid = lax.broadcasted_iota(jnp.int32, (CLIPS, QB), 0).astype(F32)
    sums = jnp.zeros((CLIPS, HD), F32)
    for j in range(WIN // QB):
        lo, hi = max(0, j * QB - ROW), min(WIN, (j + 1) * QB + ROW)
        at = slice(j * QB, (j + 1) * QB)
        qb = win[i, 0, at, :]
        ids_q = jnp.concatenate([idbuf[base + j * per + u, 0:1, :] for u in range(per)], axis=1)
        ids_q = ids_q.astype(F32)
        near_k = near[pl.ds(pl.multiple_of(start + lo, QB), hi - lo), :]
        near_q = near[pl.ds(pl.multiple_of(start + j * QB, QB), QB), :]
        s = nt(jnp.concatenate([win[i, 1, lo:hi], near_k], axis=1), jnp.concatenate([qb, near_q], axis=1))
        top = jnp.max(s, axis=0, keepdims=True)
        e = jnp.exp2((s - top) * (factor * math.log2(math.e)))
        inv = 1.0 / jnp.sum(e, axis=0, keepdims=True)
        eb = e.astype(BF16)
        o = (nn(vt[:, lo:hi], eb) * inv).T.astype(BF16).astype(F32)
        db = (dout[at, :].astype(F32) * jnp.broadcast_to(inv, (HD, QB)).T).astype(BF16)
        dp = nt(win[i, 2, lo:hi], db)
        delta = jnp.sum((db.astype(F32) * o).T, axis=0, keepdims=True)
        ds = (e * (dp - delta)).astype(BF16)
        res[i, 0, at, :] = (nn(kt[:, lo:hi], ds) * factor).T.astype(BF16)
        probs[lo:hi, at] = eb
        dscores[lo:hi, at] = ds
        dout[at, :] = db
        halo = (j * QB // ROW + parity) % 2
        inside = jnp.full((1, QB), 1 - halo, jnp.int32).astype(F32)
        good = jnp.where(ids_q != not_mine, jnp.where(ids_q == edge, 1.0, inside), 0.0)
        pick = jnp.where(cid == ids_q, good, 0.0).astype(BF16)
        prod = win[i, 3, at, :].astype(F32) * o
        ph = prod.astype(BF16)
        sums = sums + (nn(pick, ph) + nn(pick, (prod - ph.astype(F32)).astype(BF16)))
    for k0, k1 in ((0, QB), (QB, WIN - QB), (WIN - QB, WIN)):
        q0, q1 = max(0, k0 - ROW), min(WIN, k1 + ROW)
        res[i, 1, k0:k1] = (nn(dscores[k0:k1, q0:q1], win[i, 0, q0:q1]) * factor).astype(BF16)
        res[i, 2, k0:k1] = nn(probs[k0:k1, q0:q1], dout[q0:q1]).astype(BF16)
    return sums


def kernel(
    step_ref, weight_ref, q_hbm, k_hbm, v_hbm, c_hbm, ids_ref, gate_hbm,
    fin_hbm, total_ref,
    stage, src, win, res, back, idbuf, idcol, hot, near, kt, vt, dout, probs, dscores,
    gates, gate_in, sum_in, sum_out, wcol,
    load_sem, own_sem, fin_sem,
    yin_s, yin_r, zin_s, zin_r, zout_s, zout_r, yout_s, yout_r, id_s, id_r, gate_s, gate_r, sum_s, sum_r,
):
    me = lax.axis_index("seq")
    z, y = me // NY, lax.rem(me, NY)

    def ypeer(d):
        return {"seq": z * NY + lax.rem(y + d, NY)}

    def zpeer(d):
        return {"seq": lax.rem(z + d, NZ) * NY + y}

    gate_load = pltpu.make_async_copy(gate_hbm, gates, load_sem.at[4])
    loads = [
        pltpu.make_async_copy(r, stage.at[a], load_sem.at[a])
        for a, r in enumerate((q_hbm, k_hbm, v_hbm, c_hbm))
    ]
    for c in loads:
        c.start()
    gate_load.start()

    barrier = pltpu.get_barrier_semaphore()
    for d in range(1, NY):
        pl.semaphore_signal(barrier, inc=1, device_id=ypeer(d), device_id_type=MESH)
    for d in range(1, NZ):
        pl.semaphore_signal(barrier, inc=1, device_id=zpeer(d), device_id_type=MESH)

    idbuf[NY + y] = jnp.broadcast_to(ids_ref[...], (8, BLK))
    for a, c in enumerate(loads):
        c.wait()
        src[:, a] = jnp.swapaxes(stage[a], 0, 1)

    def remote(s, d, ss, rs, to):
        return pltpu.make_async_remote_copy(
            src_ref=s, dst_ref=d, send_sem=ss, recv_sem=rs, device_id=to, device_id_type=MESH
        )

    def part(first, b):
        return pl.ds(pl.multiple_of(first + b * BLK, BLK), BLK)

    def own_at(i):
        return ROW * lax.rem(i, 2)

    def yin(i, d):
        return remote(
            src.at[NY * i + lax.rem(y + d, NY)], win.at[i, :, part(own_at(i), y), :],
            yin_s.at[i, d - 1], yin_r.at[i, d - 1], ypeer(d),
        )

    def own_copy(i):
        return pltpu.make_async_copy(
            src.at[NY * i + y], win.at[i, :, part(own_at(i), y), :], own_sem.at[i]
        )

    def zin_to(i):
        return zpeer(jnp.where(lax.rem(i, 2) == 0, NZ - 1, 1))

    def zin(i, b):
        return remote(
            win.at[i, :, part(own_at(i), b), :], win.at[i, :, part(ROW - own_at(i), b), :],
            zin_s.at[i, b], zin_r.at[i, b], zin_to(i),
        )

    def zin_own(i):
        return remote(
            src.at[NY * i + y], win.at[i, :, part(ROW - own_at(i), y), :],
            zin_s.at[i, y], zin_r.at[i, y], zin_to(i),
        )

    def zout(i, b):
        return remote(
            res.at[i, :, part(ROW - own_at(i), b), :], back.at[i, :, part(0, b), :],
            zout_s.at[i, b], zout_r.at[i, b], zpeer(jnp.where(lax.rem(i, 2) == 0, 1, NZ - 1)),
        )

    def yout(i, d):
        return remote(
            res.at[i, :, part(own_at(i), lax.rem(y + d, NY)), :], fin_hbm.at[NY * i + y],
            yout_s.at[i, d - 1], yout_r.at[i, d - 1], ypeer(d),
        )

    def fin_own(i):
        return pltpu.make_async_copy(
            res.at[i, :, part(own_at(i), y), :], fin_hbm.at[NY * i + y], fin_sem.at[i]
        )

    def id_y(d):
        return remote(idbuf.at[NY + y], idbuf.at[NY + y], id_s.at[d - 1], id_r.at[d - 1], ypeer(d))

    def id_z(n):
        return remote(
            idbuf.at[pl.ds(NY, NY)], idbuf.at[pl.ds(2 * NY * n, NY)],
            id_s.at[NY - 1 + n], id_r.at[NY - 1 + n], zpeer(1 if n == 0 else NZ - 1),
        )

    def gate_copy(d):
        return remote(gate_in.at[z], gate_in.at[z], gate_s.at[d - 1], gate_r.at[d - 1], zpeer(d))

    def sum_copy(i, slot):
        return remote(
            sum_out.at[i], sum_in.at[slot], sum_s.at[i], sum_r.at[slot], zpeer(lax.rem(i - z + NZ, NZ))
        )

    def begin(i):
        for d in range(1, NY):
            yin(i, d).start()
        own_copy(i).start()

    pl.semaphore_wait(barrier, NY - 1 + NZ - 1)
    for d in range(1, NY):
        id_y(d).start()
    begin(jnp.int32(0))

    def early(i, _):
        zin_own(i).start()
        return 0

    lax.fori_loop(0, SLOTS, early, 0)
    for i in range(1, AHEAD):
        begin(jnp.int32(i))
    gate_load.wait()
    for c in range(CLIPS):
        wcol[c : c + 1, :] = jnp.full((1, HD), weight_ref[c], F32)
        gate_in[z, c : c + 1, :] = gates[pl.ds(step_ref[c], 1), :] * weight_ref[c]
    for d in range(1, NZ):
        gate_copy(d).start()
    for d in range(1, NY):
        id_y(d).wait_recv()
    for n in range(2):
        id_z(n).start()

    def step(t, _):
        @pl.when(t < SLOTS)
        def _():
            for d in range(1, NY):
                yin(t, d).wait_recv()
                zin(t, lax.rem(y + NY - d, NY)).start()
            own_copy(t).wait()

            @pl.when(t + AHEAD < SLOTS)
            def _():
                begin(t + AHEAD)

        @pl.when(t == LAG_COMPUTE)
        def _():
            for n in range(2):
                id_z(n).wait_recv()
            fill_clips(idbuf, idcol, hot, near)
            for d in range(1, NZ):
                gate_copy(d).wait_recv()

        @pl.when((t >= LAG_COMPUTE) & (t < SLOTS + LAG_COMPUTE))
        def _():
            i = t - LAG_COMPUTE
            for b in range(NY):
                zin(i, b).wait_recv()
            sums = attend(
                i, win, res, gate_in, idbuf, idcol, hot, near, kt, vt, dout, probs, dscores
            )
            for d in (1, 2, 3, 0):
                zout(i, lax.rem(y + d, NY)).start()
            sum_out[i] = sums * wcol[...]

            @pl.when(i != z)
            def _():
                sum_copy(i, z).start()

            @pl.when(i == z)
            def _():
                sum_in[z] = sum_out[i]

        @pl.when((t >= LAG_BACK) & (lax.rem(t - LAG_BACK, 2) == 0))
        def _():
            for d in (1, 2, 3, 0):
                b = lax.rem(y + d, NY)
                for odd in range(2):
                    i = t - LAG_BACK + odd
                    zout(i, b).wait_recv()
                    theirs = idcol[part(ROW, b), :] == other_clip(idcol, odd)
                    for a in range(3):
                        res[i, a, part(ROW * odd, b), :] = jnp.where(
                            theirs,
                            back[i, a, part(0, b), :].astype(F32),
                            res[i, a, part(ROW * odd, b), :].astype(F32),
                        ).astype(BF16)
                    if d:
                        yout(i, d).start()
                    else:
                        fin_own(i).start()

        return 0

    lax.fori_loop(0, SLOTS + LAG_BACK - 1, step, 0)

    def sums_arrived(i, _):
        @pl.when(i != z)
        def _():
            sum_copy(i, i).wait_recv()

        return 0

    lax.fori_loop(0, NZ, sums_arrived, 0)
    total = sum_in[0]
    for r in range(1, NZ):
        total = total + sum_in[r]
    total_ref[...] = total

    def done(i, _):
        for d in range(1, NY):
            yin(i, d).wait_send()
            yout(i, d).wait_send()
            yout(i, d).wait_recv()
        for b in range(NY):
            zin(i, b).wait_send()
            zout(i, b).wait_send()
        fin_own(i).wait()

        @pl.when(i != z)
        def _():
            sum_copy(i, z).wait_send()

        return 0

    lax.fori_loop(0, SLOTS, done, 0)
    for d in range(1, NY):
        id_y(d).wait_send()
    for n in range(2):
        id_z(n).wait_send()
    for d in range(1, NZ):
        gate_copy(d).wait_send()


def lay_out(step_ref, total_ref, fin_hbm, dq_hbm, dk_hbm, dv_hbm, table_hbm, got, put, table, in_sem, out_sem):
    half = BLK // 2
    pieces = [(a, n) for a in range(3) for n in range(2)]
    ins = [
        pltpu.make_async_copy(
            fin_hbm.at[:, a, n * half : (n + 1) * half, :], got.at[a, n], in_sem.at[a, n]
        )
        for a, n in pieces
    ]
    outs = [
        pltpu.make_async_copy(
            put.at[a, n], (dq_hbm, dk_hbm, dv_hbm)[a].at[n * half : (n + 1) * half], out_sem.at[a, n]
        )
        for a, n in pieces
    ]
    for c in ins:
        c.start()
    lane = lax.broadcasted_iota(jnp.int32, (1, HD), 1) % CLIPS
    steps = jnp.zeros((1, HD), jnp.int32)
    for c in range(CLIPS):
        steps = jnp.where(lane == c, step_ref[c], steps)
    line = lax.broadcasted_iota(jnp.int32, (STEPS, HD), 0)
    pick = jnp.where(line == steps, 1.0, 0.0).astype(BF16)
    table[...] = nn(pick, three_parts(total_ref[...]))
    table_out = pltpu.make_async_copy(table, table_hbm, out_sem.at[3, 0])
    table_out.start()
    for (a, n), i, o in zip(pieces, ins, outs):
        i.wait()
        put[a, n] = jnp.swapaxes(got[a, n], 0, 1)
        o.start()
    for o in outs:
        o.wait()
    table_out.wait()


def on_device(queries, keys, values, cotangent, clip_ids, clip_step, clip_weight, step_gate):
    vm = pl.BlockSpec(memory_space=pltpu.VMEM)
    sm = pl.BlockSpec(memory_space=pltpu.SMEM)
    hb = pl.BlockSpec(memory_space=pl.ANY)
    dma = pltpu.SemaphoreType.DMA
    fin, total = pl.pallas_call(
        kernel,
        out_shape=(
            jax.ShapeDtypeStruct((HEADS, 3, BLK, HD), BF16),
            jax.ShapeDtypeStruct((CLIPS, HD), F32),
        ),
        in_specs=[sm, sm, hb, hb, hb, hb, vm, hb],
        out_specs=(hb, vm),
        scratch_shapes=[
            pltpu.VMEM((4, BLK, HEADS, HD), BF16),
            pltpu.VMEM((HEADS, 4, BLK, HD), BF16),
            pltpu.VMEM((SLOTS, 4, WIN, HD), BF16),
            pltpu.VMEM((SLOTS, 3, WIN, HD), BF16),
            pltpu.VMEM((SLOTS, 3, ROW, HD), BF16),
            pltpu.VMEM((3 * NY, 8, BLK), jnp.int32),
            pltpu.VMEM((3 * ROW, BLK), F32),
            pltpu.VMEM((3 * ROW, HD), BF16),
            pltpu.VMEM((3 * ROW, HD), BF16),
            pltpu.VMEM((HD, WIN), BF16),
            pltpu.VMEM((HD, WIN), BF16),
            pltpu.VMEM((WIN, HD), BF16),
            pltpu.VMEM((WIN, WIN), BF16),
            pltpu.VMEM((WIN, WIN), BF16),
            pltpu.VMEM((STEPS, HD), F32),
            pltpu.VMEM((NZ, CLIPS, HD), F32),
            pltpu.VMEM((NZ, CLIPS, HD), F32),
            pltpu.VMEM((NZ, CLIPS, HD), F32),
            pltpu.VMEM((CLIPS, HD), F32),
            dma((5,)), dma((SLOTS,)), dma((SLOTS,)),
            dma((SLOTS, NY - 1)), dma((SLOTS, NY - 1)),
            dma((SLOTS, NY)), dma((SLOTS, NY)),
            dma((SLOTS, NY)), dma((SLOTS, NY)),
            dma((SLOTS, NY - 1)), dma((SLOTS, NY - 1)),
            dma((NY + 1,)), dma((NY + 1,)),
            dma((NZ - 1,)), dma((NZ - 1,)),
            dma((NZ,)), dma((NZ,)),
        ],
        compiler_params=pltpu.CompilerParams(
            collective_id=0, has_side_effects=True, vmem_limit_bytes=60 * 2**20
        ),
        cost_estimate=pl.CostEstimate(flops=12 * 2**30, bytes_accessed=8 * 2**20, transcendentals=2**23),
        name="clip_attention_backward",
    )(
        clip_step, clip_weight, queries, keys, values, cotangent,
        clip_ids.reshape(1, BLK), step_gate.reshape(STEPS, HD),
    )
    grads = jax.ShapeDtypeStruct((BLK, HEADS, HD), BF16)
    dq, dk, dv, table = pl.pallas_call(
        lay_out,
        out_shape=(grads, grads, grads, jax.ShapeDtypeStruct((STEPS, HD), F32)),
        in_specs=[sm, vm, hb],
        out_specs=(hb, hb, hb, hb),
        scratch_shapes=[
            pltpu.VMEM((3, 2, HEADS, BLK // 2, HD), BF16),
            pltpu.VMEM((3, 2, BLK // 2, HEADS, HD), BF16),
            pltpu.VMEM((STEPS, HD), F32),
            dma((3, 2)), dma((4, 2)),
        ],
        compiler_params=pltpu.CompilerParams(vmem_limit_bytes=60 * 2**20),
        cost_estimate=pl.CostEstimate(flops=2**25, bytes_accessed=7 * 2**20, transcendentals=0),
        name="lay_out",
    )(clip_step, total, fin)
    return dq, dk, dv, table.reshape(STEPS, 1, HD)


def solution(mesh):
    in_specs = (
        P(("dp", "seq"), None, None),
        P(("dp", "seq"), None, None),
        P(("dp", "seq"), None, None),
        P(("dp", "seq"), None, None),
        P(("dp", "seq")),
        P("dp"),
        P("dp"),
        P(None, "seq", None),
    )
    out_specs = (
        P(("dp", "seq"), None, None),
        P(("dp", "seq"), None, None),
        P(("dp", "seq"), None, None),
        P("dp", "seq", None),
    )
    return jax.shard_map(
        on_device, mesh=mesh, in_specs=in_specs, out_specs=out_specs, check_vma=False
    )
```

```python
import math

import jax
import jax.numpy as jnp
from jax import lax
from jax.experimental import pallas as pl
from jax.experimental.pallas import tpu as pltpu
from jax.sharding import PartitionSpec as P

NY = 4
NZ = 8
BLK = 128
ROW = NY * BLK
WIN = 2 * ROW
HD = 128
HEADS = 32
SLOTS = HEADS // NY
CLIPS = 16
STEPS = 1000
QB = 256
NEAR = 80.0
AHEAD = 2
FIRST = (0, 1, 2, 3, 5, 7)
LATER = ((4, 0), (6, 2))
LAG_COMPUTE = 3
LAG_BACK = 7
MESH = pl.DeviceIdType.MESH
F32 = jnp.float32
BF16 = jnp.bfloat16


def nt(a, b):
    return lax.dot_general(a, b, (((1,), (1,)), ((), ())), preferred_element_type=F32)


def nn(a, b):
    return jnp.dot(a, b, preferred_element_type=F32)


def fill_clips(idbuf, idcol, hot, near):
    lane = lax.broadcasted_iota(jnp.int32, (BLK, HD), 1)
    clip = (lane % CLIPS).astype(F32)
    once = jnp.where(lane < CLIPS, NEAR, 0.0)

    def one(b, _):
        at = pl.ds(pl.multiple_of(b * BLK, BLK), BLK)
        ids = jnp.broadcast_to(idbuf[b, 0:1, :].astype(F32), (BLK, BLK)).T
        idcol[at, :] = ids
        hot[at, :] = jnp.where(ids == clip, 1.0, 0.0).astype(BF16)
        near[at, :] = jnp.where(ids == clip, once, 0.0).astype(BF16)
        return 0

    lax.fori_loop(0, 3 * NY, one, 0)


def three_parts(x):
    hi = x.astype(BF16)
    rest = x - hi.astype(F32)
    mid = rest.astype(BF16)
    low = (rest - mid.astype(F32)).astype(BF16)
    return jnp.concatenate([hi, mid, low, jnp.zeros((HD - 3 * CLIPS, HD), BF16)], axis=0)


def other_clip(idcol, parity):
    return idcol[pl.ds(2 * ROW - (ROW + 1) * (1 - parity), 1), :]


def attend(i, win, res, gate_in, idbuf, idcol, hot, near, kt, vt, dout, probs, dscores):
    parity = lax.rem(i, 2)
    base = NY * (1 - parity)
    start = pl.multiple_of(base * BLK, BLK)
    kt[...] = win[i, 1].T
    vt[...] = win[i, 2].T
    scale = nn(hot[pl.ds(start, WIN), :], three_parts(gate_in[i]))
    dout[...] = (scale * win[i, 3].astype(F32)).astype(BF16)

    factor = 1.0 / math.sqrt(HD)
    per = QB // BLK
    not_mine = jnp.concatenate([other_clip(idcol, parity)] * per, axis=1)
    edge = jnp.concatenate([idcol[pl.ds(2 * ROW - ROW * parity - (1 - parity), 1), :]] * per, axis=1)
    cid = lax.broadcasted_iota(jnp.int32, (CLIPS, QB), 0).astype(F32)
    sums = jnp.zeros((CLIPS, HD), F32)
    for j in range(WIN // QB):
        lo, hi = max(0, j * QB - ROW), min(WIN, (j + 1) * QB + ROW)
        at = slice(j * QB, (j + 1) * QB)
        qb = win[i, 0, at, :]
        ids_q = jnp.concatenate([idbuf[base + j * per + u, 0:1, :] for u in range(per)], axis=1)
        ids_q = ids_q.astype(F32)
        near_k = near[pl.ds(pl.multiple_of(start + lo, QB), hi - lo), :]
        near_q = near[pl.ds(pl.multiple_of(start + j * QB, QB), QB), :]
        s = nt(jnp.concatenate([win[i, 1, lo:hi], near_k], axis=1), jnp.concatenate([qb, near_q], axis=1))
        top = jnp.max(s, axis=0, keepdims=True)
        e = jnp.exp2((s - top) * (factor * math.log2(math.e)))
        inv = 1.0 / jnp.sum(e, axis=0, keepdims=True)
        eb = e.astype(BF16)
        o = (nn(vt[:, lo:hi], eb) * inv).T.astype(BF16).astype(F32)
        db = (dout[at, :].astype(F32) * jnp.broadcast_to(inv, (HD, QB)).T).astype(BF16)
        dp = nt(win[i, 2, lo:hi], db)
        delta = jnp.sum((db.astype(F32) * o).T, axis=0, keepdims=True)
        ds = (e * (dp - delta)).astype(BF16)
        res[i, 0, at, :] = (nn(kt[:, lo:hi], ds) * factor).T.astype(BF16)
        probs[lo:hi, at] = eb
        dscores[lo:hi, at] = ds
        dout[at, :] = db
        halo = (j * QB // ROW + parity) % 2
        inside = jnp.full((1, QB), 1 - halo, jnp.int32).astype(F32)
        good = jnp.where(ids_q != not_mine, jnp.where(ids_q == edge, 1.0, inside), 0.0)
        pick = jnp.where(cid == ids_q, good, 0.0).astype(BF16)
        prod = win[i, 3, at, :].astype(F32) * o
        ph = prod.astype(BF16)
        sums = sums + (nn(pick, ph) + nn(pick, (prod - ph.astype(F32)).astype(BF16)))
    for k0, k1 in ((0, QB), (QB, WIN - QB), (WIN - QB, WIN)):
        q0, q1 = max(0, k0 - ROW), min(WIN, k1 + ROW)
        res[i, 1, k0:k1] = (nn(dscores[k0:k1, q0:q1], win[i, 0, q0:q1]) * factor).astype(BF16)
        res[i, 2, k0:k1] = nn(probs[k0:k1, q0:q1], dout[q0:q1]).astype(BF16)
    return sums


def kernel(
    step_ref, weight_ref, q_hbm, k_hbm, v_hbm, c_hbm, ids_ref, gate_hbm,
    fin_hbm, total_ref,
    stage, src, win, res, back, idbuf, idcol, hot, near, kt, vt, dout, probs, dscores,
    gates, gate_in, sum_in, sum_out, wcol,
    load_sem, own_sem, fin_sem,
    yin_s, yin_r, zin_s, zin_r, zout_s, zout_r, yout_s, yout_r, id_s, id_r, gate_s, gate_r, sum_s, sum_r,
):
    me = lax.axis_index("seq")
    z, y = me // NY, lax.rem(me, NY)

    def ypeer(d):
        return {"seq": z * NY + lax.rem(y + d, NY)}

    def zpeer(d):
        return {"seq": lax.rem(z + d, NZ) * NY + y}

    gate_load = pltpu.make_async_copy(gate_hbm, gates, load_sem.at[4])
    loads = [
        pltpu.make_async_copy(r, stage.at[a], load_sem.at[a])
        for a, r in enumerate((q_hbm, k_hbm, v_hbm, c_hbm))
    ]
    for c in loads:
        c.start()
    gate_load.start()

    barrier = pltpu.get_barrier_semaphore()
    for d in range(1, NY):
        pl.semaphore_signal(barrier, inc=1, device_id=ypeer(d), device_id_type=MESH)
    for d in range(1, NZ):
        pl.semaphore_signal(barrier, inc=1, device_id=zpeer(d), device_id_type=MESH)

    idbuf[NY + y] = jnp.broadcast_to(ids_ref[...], (8, BLK))
    for a, c in enumerate(loads):
        c.wait()
        src[:, a] = jnp.swapaxes(stage[a], 0, 1)

    def remote(s, d, ss, rs, to):
        return pltpu.make_async_remote_copy(
            src_ref=s, dst_ref=d, send_sem=ss, recv_sem=rs, device_id=to, device_id_type=MESH
        )

    def part(first, b):
        return pl.ds(pl.multiple_of(first + b * BLK, BLK), BLK)

    def own_at(i):
        return ROW * lax.rem(i, 2)

    def yin(i, d):
        return remote(
            src.at[NY * i + lax.rem(y + d, NY)], win.at[i, :, part(own_at(i), y), :],
            yin_s.at[i, d - 1], yin_r.at[i, d - 1], ypeer(d),
        )

    def own_copy(i):
        return pltpu.make_async_copy(
            src.at[NY * i + y], win.at[i, :, part(own_at(i), y), :], own_sem.at[i]
        )

    def zin_to(i):
        return zpeer(jnp.where(lax.rem(i, 2) == 0, NZ - 1, 1))

    def zin(i, b):
        return remote(
            win.at[i, :, part(own_at(i), b), :], win.at[i, :, part(ROW - own_at(i), b), :],
            zin_s.at[i, b], zin_r.at[i, b], zin_to(i),
        )

    def zin_own(i):
        return remote(
            src.at[NY * i + y], win.at[i, :, part(ROW - own_at(i), y), :],
            zin_s.at[i, y], zin_r.at[i, y], zin_to(i),
        )

    def zout(i, b):
        return remote(
            res.at[i, :, part(ROW - own_at(i), b), :], back.at[i, :, part(0, b), :],
            zout_s.at[i, b], zout_r.at[i, b], zpeer(jnp.where(lax.rem(i, 2) == 0, 1, NZ - 1)),
        )

    def yout(i, d):
        return remote(
            res.at[i, :, part(own_at(i), lax.rem(y + d, NY)), :], fin_hbm.at[NY * i + y],
            yout_s.at[i, d - 1], yout_r.at[i, d - 1], ypeer(d),
        )

    def fin_own(i):
        return pltpu.make_async_copy(
            res.at[i, :, part(own_at(i), y), :], fin_hbm.at[NY * i + y], fin_sem.at[i]
        )

    def id_y(d):
        return remote(idbuf.at[NY + y], idbuf.at[NY + y], id_s.at[d - 1], id_r.at[d - 1], ypeer(d))

    def id_z(n):
        return remote(
            idbuf.at[pl.ds(NY, NY)], idbuf.at[pl.ds(2 * NY * n, NY)],
            id_s.at[NY - 1 + n], id_r.at[NY - 1 + n], zpeer(1 if n == 0 else NZ - 1),
        )

    def gate_copy(d):
        return remote(gate_in.at[z], gate_in.at[z], gate_s.at[d - 1], gate_r.at[d - 1], zpeer(d))

    def sum_copy(i, slot):
        return remote(
            sum_out.at[i], sum_in.at[slot], sum_s.at[i], sum_r.at[slot], zpeer(lax.rem(i - z + NZ, NZ))
        )

    def begin(i):
        for d in range(1, NY):
            yin(i, d).start()
        own_copy(i).start()

    pl.semaphore_wait(barrier, NY - 1 + NZ - 1)
    for d in range(1, NY):
        id_y(d).start()
    begin(jnp.int32(0))

    for i in FIRST:
        zin_own(jnp.int32(i)).start()
    for i in range(1, AHEAD):
        begin(jnp.int32(i))
    gate_load.wait()
    for c in range(CLIPS):
        wcol[c : c + 1, :] = jnp.full((1, HD), weight_ref[c], F32)
        gate_in[z, c : c + 1, :] = gates[pl.ds(step_ref[c], 1), :] * weight_ref[c]
    for d in range(1, NZ):
        gate_copy(d).start()
    for d in range(1, NY):
        id_y(d).wait_recv()
    for n in range(2):
        id_z(n).start()

    def step(t, _):
        @pl.when(t < SLOTS)
        def _():
            for d in range(1, NY):
                yin(t, d).wait_recv()
                zin(t, lax.rem(y + NY - d, NY)).start()
            own_copy(t).wait()
            for i, after in LATER:

                @pl.when(t == after)
                def _():
                    zin_own(jnp.int32(i)).start()

            @pl.when(t + AHEAD < SLOTS)
            def _():
                begin(t + AHEAD)

        @pl.when(t == 1)
        def _():
            for n in range(2):
                id_z(n).wait_recv()
            fill_clips(idbuf, idcol, hot, near)
            for d in range(1, NZ):
                gate_copy(d).wait_recv()

        @pl.when((t >= LAG_COMPUTE) & (t < SLOTS + LAG_COMPUTE))
        def _():
            i = t - LAG_COMPUTE
            for b in range(NY):
                zin(i, b).wait_recv()
            sums = attend(
                i, win, res, gate_in, idbuf, idcol, hot, near, kt, vt, dout, probs, dscores
            )
            for d in (1, 2, 3, 0):
                zout(i, lax.rem(y + d, NY)).start()
            sum_out[i] = sums * wcol[...]

            @pl.when(i != z)
            def _():
                sum_copy(i, z).start()

            @pl.when(i == z)
            def _():
                sum_in[z] = sum_out[i]

        @pl.when((t >= LAG_BACK) & (lax.rem(t - LAG_BACK, 2) == 0))
        def _():
            for d in (1, 2, 3, 0):
                b = lax.rem(y + d, NY)
                for odd in range(2):
                    i = t - LAG_BACK + odd
                    zout(i, b).wait_recv()
                    theirs = idcol[part(ROW, b), :] == other_clip(idcol, odd)
                    for a in range(3):
                        res[i, a, part(ROW * odd, b), :] = jnp.where(
                            theirs,
                            back[i, a, part(0, b), :].astype(F32),
                            res[i, a, part(ROW * odd, b), :].astype(F32),
                        ).astype(BF16)
                    if d:
                        yout(i, d).start()
                    else:
                        fin_own(i).start()

        return 0

    lax.fori_loop(0, SLOTS + LAG_BACK - 1, step, 0)

    def sums_arrived(i, _):
        @pl.when(i != z)
        def _():
            sum_copy(i, i).wait_recv()

        return 0

    lax.fori_loop(0, NZ, sums_arrived, 0)
    total = sum_in[0]
    for r in range(1, NZ):
        total = total + sum_in[r]
    total_ref[...] = total

    def done(i, _):
        for d in range(1, NY):
            yin(i, d).wait_send()
            yout(i, d).wait_send()
            yout(i, d).wait_recv()
        for b in range(NY):
            zin(i, b).wait_send()
            zout(i, b).wait_send()
        fin_own(i).wait()

        @pl.when(i != z)
        def _():
            sum_copy(i, z).wait_send()

        return 0

    lax.fori_loop(0, SLOTS, done, 0)
    for d in range(1, NY):
        id_y(d).wait_send()
    for n in range(2):
        id_z(n).wait_send()
    for d in range(1, NZ):
        gate_copy(d).wait_send()


def lay_out(step_ref, total_ref, fin_hbm, dq_hbm, dk_hbm, dv_hbm, table_hbm, got, put, table, in_sem, out_sem):
    half = BLK // 2
    pieces = [(a, n) for a in range(3) for n in range(2)]
    ins = [
        pltpu.make_async_copy(
            fin_hbm.at[:, a, n * half : (n + 1) * half, :], got.at[a, n], in_sem.at[a, n]
        )
        for a, n in pieces
    ]
    outs = [
        pltpu.make_async_copy(
            put.at[a, n], (dq_hbm, dk_hbm, dv_hbm)[a].at[n * half : (n + 1) * half], out_sem.at[a, n]
        )
        for a, n in pieces
    ]
    for c in ins:
        c.start()
    lane = lax.broadcasted_iota(jnp.int32, (1, HD), 1) % CLIPS
    steps = jnp.zeros((1, HD), jnp.int32)
    for c in range(CLIPS):
        steps = jnp.where(lane == c, step_ref[c], steps)
    line = lax.broadcasted_iota(jnp.int32, (STEPS, HD), 0)
    pick = jnp.where(line == steps, 1.0, 0.0).astype(BF16)
    table[...] = nn(pick, three_parts(total_ref[...]))
    table_out = pltpu.make_async_copy(table, table_hbm, out_sem.at[3, 0])
    table_out.start()
    for (a, n), i, o in zip(pieces, ins, outs):
        i.wait()
        put[a, n] = jnp.swapaxes(got[a, n], 0, 1)
        o.start()
    for o in outs:
        o.wait()
    table_out.wait()


def on_device(queries, keys, values, cotangent, clip_ids, clip_step, clip_weight, step_gate):
    vm = pl.BlockSpec(memory_space=pltpu.VMEM)
    sm = pl.BlockSpec(memory_space=pltpu.SMEM)
    hb = pl.BlockSpec(memory_space=pl.ANY)
    dma = pltpu.SemaphoreType.DMA
    fin, total = pl.pallas_call(
        kernel,
        out_shape=(
            jax.ShapeDtypeStruct((HEADS, 3, BLK, HD), BF16),
            jax.ShapeDtypeStruct((CLIPS, HD), F32),
        ),
        in_specs=[sm, sm, hb, hb, hb, hb, vm, hb],
        out_specs=(hb, vm),
        scratch_shapes=[
            pltpu.VMEM((4, BLK, HEADS, HD), BF16),
            pltpu.VMEM((HEADS, 4, BLK, HD), BF16),
            pltpu.VMEM((SLOTS, 4, WIN, HD), BF16),
            pltpu.VMEM((SLOTS, 3, WIN, HD), BF16),
            pltpu.VMEM((SLOTS, 3, ROW, HD), BF16),
            pltpu.VMEM((3 * NY, 8, BLK), jnp.int32),
            pltpu.VMEM((3 * ROW, BLK), F32),
            pltpu.VMEM((3 * ROW, HD), BF16),
            pltpu.VMEM((3 * ROW, HD), BF16),
            pltpu.VMEM((HD, WIN), BF16),
            pltpu.VMEM((HD, WIN), BF16),
            pltpu.VMEM((WIN, HD), BF16),
            pltpu.VMEM((WIN, WIN), BF16),
            pltpu.VMEM((WIN, WIN), BF16),
            pltpu.VMEM((STEPS, HD), F32),
            pltpu.VMEM((NZ, CLIPS, HD), F32),
            pltpu.VMEM((NZ, CLIPS, HD), F32),
            pltpu.VMEM((NZ, CLIPS, HD), F32),
            pltpu.VMEM((CLIPS, HD), F32),
            dma((5,)), dma((SLOTS,)), dma((SLOTS,)),
            dma((SLOTS, NY - 1)), dma((SLOTS, NY - 1)),
            dma((SLOTS, NY)), dma((SLOTS, NY)),
            dma((SLOTS, NY)), dma((SLOTS, NY)),
            dma((SLOTS, NY - 1)), dma((SLOTS, NY - 1)),
            dma((NY + 1,)), dma((NY + 1,)),
            dma((NZ - 1,)), dma((NZ - 1,)),
            dma((NZ,)), dma((NZ,)),
        ],
        compiler_params=pltpu.CompilerParams(
            collective_id=0, has_side_effects=True, vmem_limit_bytes=60 * 2**20
        ),
        cost_estimate=pl.CostEstimate(flops=12 * 2**30, bytes_accessed=8 * 2**20, transcendentals=2**23),
        name="clip_attention_backward",
    )(
        clip_step, clip_weight, queries, keys, values, cotangent,
        clip_ids.reshape(1, BLK), step_gate.reshape(STEPS, HD),
    )
    grads = jax.ShapeDtypeStruct((BLK, HEADS, HD), BF16)
    dq, dk, dv, table = pl.pallas_call(
        lay_out,
        out_shape=(grads, grads, grads, jax.ShapeDtypeStruct((STEPS, HD), F32)),
        in_specs=[sm, vm, hb],
        out_specs=(hb, hb, hb, hb),
        scratch_shapes=[
            pltpu.VMEM((3, 2, HEADS, BLK // 2, HD), BF16),
            pltpu.VMEM((3, 2, BLK // 2, HEADS, HD), BF16),
            pltpu.VMEM((STEPS, HD), F32),
            dma((3, 2)), dma((4, 2)),
        ],
        compiler_params=pltpu.CompilerParams(vmem_limit_bytes=60 * 2**20),
        cost_estimate=pl.CostEstimate(flops=2**25, bytes_accessed=7 * 2**20, transcendentals=0),
        name="lay_out",
    )(clip_step, total, fin)
    return dq, dk, dv, table.reshape(STEPS, 1, HD)


def solution(mesh):
    in_specs = (
        P(("dp", "seq"), None, None),
        P(("dp", "seq"), None, None),
        P(("dp", "seq"), None, None),
        P(("dp", "seq"), None, None),
        P(("dp", "seq")),
        P("dp"),
        P("dp"),
        P(None, "seq", None),
    )
    out_specs = (
        P(("dp", "seq"), None, None),
        P(("dp", "seq"), None, None),
        P(("dp", "seq"), None, None),
        P("dp", "seq", None),
    )
    return jax.shard_map(
        on_device, mesh=mesh, in_specs=in_specs, out_specs=out_specs, check_vma=False
    )
```

```python
import math

import jax
import jax.numpy as jnp
from jax import lax
from jax.experimental import pallas as pl
from jax.experimental.pallas import tpu as pltpu
from jax.sharding import PartitionSpec as P

NY = 4
NZ = 8
BLK = 128
ROW = NY * BLK
WIN = 2 * ROW
HD = 128
HEADS = 32
SLOTS = HEADS // NY
CLIPS = 16
STEPS = 1000
QB = 256
NEAR = 80.0
AHEAD = 2
FIRST = (0, 1, 2, 3, 5, 7)
LATER = ((4, 0), (6, 2))
LAG_COMPUTE = 3
LAG_BACK = 8
MESH = pl.DeviceIdType.MESH
F32 = jnp.float32
BF16 = jnp.bfloat16


def nt(a, b):
    return lax.dot_general(a, b, (((1,), (1,)), ((), ())), preferred_element_type=F32)


def nn(a, b):
    return jnp.dot(a, b, preferred_element_type=F32)


def fill_clips(idbuf, idcol, hot, near):
    lane = lax.broadcasted_iota(jnp.int32, (BLK, HD), 1)
    clip = (lane % CLIPS).astype(F32)
    once = jnp.where(lane < CLIPS, NEAR, 0.0)

    def one(b, _):
        at = pl.ds(pl.multiple_of(b * BLK, BLK), BLK)
        ids = jnp.broadcast_to(idbuf[b, 0:1, :].astype(F32), (BLK, BLK)).T
        idcol[at, :] = ids
        hot[at, :] = jnp.where(ids == clip, 1.0, 0.0).astype(BF16)
        near[at, :] = jnp.where(ids == clip, once, 0.0).astype(BF16)
        return 0

    lax.fori_loop(0, 3 * NY, one, 0)


def three_parts(x):
    hi = x.astype(BF16)
    rest = x - hi.astype(F32)
    mid = rest.astype(BF16)
    low = (rest - mid.astype(F32)).astype(BF16)
    return jnp.concatenate([hi, mid, low, jnp.zeros((HD - 3 * CLIPS, HD), BF16)], axis=0)


def other_clip(idcol, parity):
    return idcol[pl.ds(2 * ROW - (ROW + 1) * (1 - parity), 1), :]


def attend(i, win, res, gate_in, idbuf, idcol, hot, near, kt, vt, dout, probs, dscores):
    parity = lax.rem(i, 2)
    base = NY * (1 - parity)
    start = pl.multiple_of(base * BLK, BLK)
    kt[...] = win[i, 1].T
    vt[...] = win[i, 2].T
    scale = nn(hot[pl.ds(start, WIN), :], three_parts(gate_in[i]))
    dout[...] = (scale * win[i, 3].astype(F32)).astype(BF16)

    factor = 1.0 / math.sqrt(HD)
    per = QB // BLK
    not_mine = jnp.concatenate([other_clip(idcol, parity)] * per, axis=1)
    edge = jnp.concatenate([idcol[pl.ds(2 * ROW - ROW * parity - (1 - parity), 1), :]] * per, axis=1)
    cid = lax.broadcasted_iota(jnp.int32, (CLIPS, QB), 0).astype(F32)
    sums = jnp.zeros((CLIPS, HD), F32)
    for j in range(WIN // QB):
        lo, hi = max(0, j * QB - ROW), min(WIN, (j + 1) * QB + ROW)
        at = slice(j * QB, (j + 1) * QB)
        qb = win[i, 0, at, :]
        ids_q = jnp.concatenate([idbuf[base + j * per + u, 0:1, :] for u in range(per)], axis=1)
        ids_q = ids_q.astype(F32)
        near_k = near[pl.ds(pl.multiple_of(start + lo, QB), hi - lo), :]
        near_q = near[pl.ds(pl.multiple_of(start + j * QB, QB), QB), :]
        s = nt(jnp.concatenate([win[i, 1, lo:hi], near_k], axis=1), jnp.concatenate([qb, near_q], axis=1))
        top = jnp.max(s, axis=0, keepdims=True)
        e = jnp.exp2((s - top) * (factor * math.log2(math.e)))
        inv = 1.0 / jnp.sum(e, axis=0, keepdims=True)
        eb = e.astype(BF16)
        o = (nn(vt[:, lo:hi], eb) * inv).T.astype(BF16).astype(F32)
        db = (dout[at, :].astype(F32) * jnp.broadcast_to(inv, (HD, QB)).T).astype(BF16)
        dp = nt(win[i, 2, lo:hi], db)
        delta = jnp.sum((db.astype(F32) * o).T, axis=0, keepdims=True)
        ds = (e * (dp - delta)).astype(BF16)
        res[i, 0, at, :] = (nn(kt[:, lo:hi], ds) * factor).T.astype(BF16)
        probs[lo:hi, at] = eb
        dscores[lo:hi, at] = ds
        dout[at, :] = db
        halo = (j * QB // ROW + parity) % 2
        inside = jnp.full((1, QB), 1 - halo, jnp.int32).astype(F32)
        good = jnp.where(ids_q != not_mine, jnp.where(ids_q == edge, 1.0, inside), 0.0)
        pick = jnp.where(cid == ids_q, good, 0.0).astype(BF16)
        prod = win[i, 3, at, :].astype(F32) * o
        ph = prod.astype(BF16)
        sums = sums + (nn(pick, ph) + nn(pick, (prod - ph.astype(F32)).astype(BF16)))
    for k0, k1 in ((0, QB), (QB, WIN - QB), (WIN - QB, WIN)):
        q0, q1 = max(0, k0 - ROW), min(WIN, k1 + ROW)
        res[i, 1, k0:k1] = (nn(dscores[k0:k1, q0:q1], win[i, 0, q0:q1]) * factor).astype(BF16)
        res[i, 2, k0:k1] = nn(probs[k0:k1, q0:q1], dout[q0:q1]).astype(BF16)
    return sums


def kernel(
    step_ref, weight_ref, q_hbm, k_hbm, v_hbm, c_hbm, ids_ref, gate_hbm,
    fin_hbm, total_ref,
    stage, src, win, res, back, idbuf, idcol, hot, near, kt, vt, dout, probs, dscores,
    gates, gate_in, sum_in, sum_out, wcol,
    load_sem, own_sem, fin_sem,
    yin_s, yin_r, zin_s, zin_r, zout_s, zout_r, yout_s, yout_r, id_s, id_r, gate_s, gate_r, sum_s, sum_r,
):
    me = lax.axis_index("seq")
    z, y = me // NY, lax.rem(me, NY)

    def ypeer(d):
        return {"seq": z * NY + lax.rem(y + d, NY)}

    def zpeer(d):
        return {"seq": lax.rem(z + d, NZ) * NY + y}

    gate_load = pltpu.make_async_copy(gate_hbm, gates, load_sem.at[4])
    loads = [
        pltpu.make_async_copy(r, stage.at[a], load_sem.at[a])
        for a, r in enumerate((q_hbm, k_hbm, v_hbm, c_hbm))
    ]
    for c in loads:
        c.start()
    gate_load.start()

    barrier = pltpu.get_barrier_semaphore()
    for d in range(1, NY):
        pl.semaphore_signal(barrier, inc=1, device_id=ypeer(d), device_id_type=MESH)
    for d in range(1, NZ):
        pl.semaphore_signal(barrier, inc=1, device_id=zpeer(d), device_id_type=MESH)

    idbuf[NY + y] = jnp.broadcast_to(ids_ref[...], (8, BLK))
    for a, c in enumerate(loads):
        c.wait()
        src[:, a] = jnp.swapaxes(stage[a], 0, 1)

    def remote(s, d, ss, rs, to):
        return pltpu.make_async_remote_copy(
            src_ref=s, dst_ref=d, send_sem=ss, recv_sem=rs, device_id=to, device_id_type=MESH
        )

    def part(first, b):
        return pl.ds(pl.multiple_of(first + b * BLK, BLK), BLK)

    def own_at(i):
        return ROW * lax.rem(i, 2)

    def yin(i, d):
        return remote(
            src.at[NY * i + lax.rem(y + d, NY)], win.at[i, :, part(own_at(i), y), :],
            yin_s.at[i, d - 1], yin_r.at[i, d - 1], ypeer(d),
        )

    def own_copy(i):
        return pltpu.make_async_copy(
            src.at[NY * i + y], win.at[i, :, part(own_at(i), y), :], own_sem.at[i]
        )

    def zin_to(i):
        return zpeer(jnp.where(lax.rem(i, 2) == 0, NZ - 1, 1))

    def zin(i, b):
        return remote(
            win.at[i, :, part(own_at(i), b), :], win.at[i, :, part(ROW - own_at(i), b), :],
            zin_s.at[i, b], zin_r.at[i, b], zin_to(i),
        )

    def zin_own(i):
        return remote(
            src.at[NY * i + y], win.at[i, :, part(ROW - own_at(i), y), :],
            zin_s.at[i, y], zin_r.at[i, y], zin_to(i),
        )

    def zout(i, b):
        return remote(
            res.at[i, :, part(ROW - own_at(i), b), :], back.at[i, :, part(0, b), :],
            zout_s.at[i, b], zout_r.at[i, b], zpeer(jnp.where(lax.rem(i, 2) == 0, 1, NZ - 1)),
        )

    def yout(i, d):
        return remote(
            res.at[i, :, part(own_at(i), lax.rem(y + d, NY)), :], fin_hbm.at[NY * i + y],
            yout_s.at[i, d - 1], yout_r.at[i, d - 1], ypeer(d),
        )

    def fin_own(i):
        return pltpu.make_async_copy(
            res.at[i, :, part(own_at(i), y), :], fin_hbm.at[NY * i + y], fin_sem.at[i]
        )

    def id_y(d):
        return remote(idbuf.at[NY + y], idbuf.at[NY + y], id_s.at[d - 1], id_r.at[d - 1], ypeer(d))

    def id_z(n):
        return remote(
            idbuf.at[pl.ds(NY, NY)], idbuf.at[pl.ds(2 * NY * n, NY)],
            id_s.at[NY - 1 + n], id_r.at[NY - 1 + n], zpeer(1 if n == 0 else NZ - 1),
        )

    def gate_copy(d):
        return remote(gate_in.at[z], gate_in.at[z], gate_s.at[d - 1], gate_r.at[d - 1], zpeer(d))

    def sum_copy(i, slot):
        return remote(
            sum_out.at[i], sum_in.at[slot], sum_s.at[i], sum_r.at[slot], zpeer(lax.rem(i - z + NZ, NZ))
        )

    def begin(i):
        for d in range(1, NY):
            yin(i, d).start()
        own_copy(i).start()

    pl.semaphore_wait(barrier, NY - 1 + NZ - 1)
    for d in range(1, NY):
        id_y(d).start()
    begin(jnp.int32(0))

    for i in FIRST:
        zin_own(jnp.int32(i)).start()
    for i in range(1, AHEAD):
        begin(jnp.int32(i))
    gate_load.wait()
    for c in range(CLIPS):
        wcol[c : c + 1, :] = jnp.full((1, HD), weight_ref[c], F32)
        gate_in[z, c : c + 1, :] = gates[pl.ds(step_ref[c], 1), :] * weight_ref[c]
    for d in range(1, NZ):
        gate_copy(d).start()
    for d in range(1, NY):
        id_y(d).wait_recv()
    for n in range(2):
        id_z(n).start()

    def step(t, _):
        @pl.when(t < SLOTS)
        def _():
            for d in range(1, NY):
                yin(t, d).wait_recv()
                zin(t, lax.rem(y + NY - d, NY)).start()
            own_copy(t).wait()
            for i, after in LATER:

                @pl.when(t == after)
                def _():
                    zin_own(jnp.int32(i)).start()

            @pl.when(t + AHEAD < SLOTS)
            def _():
                begin(t + AHEAD)

        @pl.when(t == 1)
        def _():
            for n in range(2):
                id_z(n).wait_recv()
            fill_clips(idbuf, idcol, hot, near)
            for d in range(1, NZ):
                gate_copy(d).wait_recv()

        @pl.when((t >= LAG_COMPUTE) & (t < SLOTS + LAG_COMPUTE))
        def _():
            i = t - LAG_COMPUTE
            for b in range(NY):
                zin(i, b).wait_recv()
            sums = attend(
                i, win, res, gate_in, idbuf, idcol, hot, near, kt, vt, dout, probs, dscores
            )
            for d in (1, 2, 3, 0):
                zout(i, lax.rem(y + d, NY)).start()
            sum_out[i] = sums * wcol[...]

            @pl.when(i != z)
            def _():
                sum_copy(i, z).start()

            @pl.when(i == z)
            def _():
                sum_in[z] = sum_out[i]

        @pl.when((t >= LAG_BACK) & (lax.rem(t - LAG_BACK, 2) == 0))
        def _():
            for d in (1, 2, 3, 0):
                b = lax.rem(y + d, NY)
                for odd in range(2):
                    i = t - LAG_BACK + odd
                    zout(i, b).wait_recv()
                    theirs = idcol[part(ROW, b), :] == other_clip(idcol, odd)
                    for a in range(3):
                        res[i, a, part(ROW * odd, b), :] = jnp.where(
                            theirs,
                            back[i, a, part(0, b), :].astype(F32),
                            res[i, a, part(ROW * odd, b), :].astype(F32),
                        ).astype(BF16)
                    if d:
                        yout(i, d).start()
                    else:
                        fin_own(i).start()

        return 0

    lax.fori_loop(0, SLOTS + LAG_BACK - 1, step, 0)

    def sums_arrived(i, _):
        @pl.when(i != z)
        def _():
            sum_copy(i, i).wait_recv()

        return 0

    lax.fori_loop(0, NZ, sums_arrived, 0)
    total = sum_in[0]
    for r in range(1, NZ):
        total = total + sum_in[r]
    total_ref[...] = total

    def done(i, _):
        for d in range(1, NY):
            yin(i, d).wait_send()
            yout(i, d).wait_send()
            yout(i, d).wait_recv()
        for b in range(NY):
            zin(i, b).wait_send()
            zout(i, b).wait_send()
        fin_own(i).wait()

        @pl.when(i != z)
        def _():
            sum_copy(i, z).wait_send()

        return 0

    lax.fori_loop(0, SLOTS, done, 0)
    for d in range(1, NY):
        id_y(d).wait_send()
    for n in range(2):
        id_z(n).wait_send()
    for d in range(1, NZ):
        gate_copy(d).wait_send()


def lay_out(step_ref, total_ref, fin_hbm, dq_hbm, dk_hbm, dv_hbm, table_hbm, got, put, table, in_sem, out_sem):
    half = BLK // 2
    pieces = [(a, n) for a in range(3) for n in range(2)]
    ins = [
        pltpu.make_async_copy(
            fin_hbm.at[:, a, n * half : (n + 1) * half, :], got.at[a, n], in_sem.at[a, n]
        )
        for a, n in pieces
    ]
    outs = [
        pltpu.make_async_copy(
            put.at[a, n], (dq_hbm, dk_hbm, dv_hbm)[a].at[n * half : (n + 1) * half], out_sem.at[a, n]
        )
        for a, n in pieces
    ]
    for c in ins:
        c.start()
    lane = lax.broadcasted_iota(jnp.int32, (1, HD), 1) % CLIPS
    steps = jnp.zeros((1, HD), jnp.int32)
    for c in range(CLIPS):
        steps = jnp.where(lane == c, step_ref[c], steps)
    line = lax.broadcasted_iota(jnp.int32, (STEPS, HD), 0)
    pick = jnp.where(line == steps, 1.0, 0.0).astype(BF16)
    table[...] = nn(pick, three_parts(total_ref[...]))
    table_out = pltpu.make_async_copy(table, table_hbm, out_sem.at[3, 0])
    table_out.start()
    for (a, n), i, o in zip(pieces, ins, outs):
        i.wait()
        put[a, n] = jnp.swapaxes(got[a, n], 0, 1)
        o.start()
    for o in outs:
        o.wait()
    table_out.wait()


def on_device(queries, keys, values, cotangent, clip_ids, clip_step, clip_weight, step_gate):
    vm = pl.BlockSpec(memory_space=pltpu.VMEM)
    sm = pl.BlockSpec(memory_space=pltpu.SMEM)
    hb = pl.BlockSpec(memory_space=pl.ANY)
    dma = pltpu.SemaphoreType.DMA
    fin, total = pl.pallas_call(
        kernel,
        out_shape=(
            jax.ShapeDtypeStruct((HEADS, 3, BLK, HD), BF16),
            jax.ShapeDtypeStruct((CLIPS, HD), F32),
        ),
        in_specs=[sm, sm, hb, hb, hb, hb, vm, hb],
        out_specs=(hb, vm),
        scratch_shapes=[
            pltpu.VMEM((4, BLK, HEADS, HD), BF16),
            pltpu.VMEM((HEADS, 4, BLK, HD), BF16),
            pltpu.VMEM((SLOTS, 4, WIN, HD), BF16),
            pltpu.VMEM((SLOTS, 3, WIN, HD), BF16),
            pltpu.VMEM((SLOTS, 3, ROW, HD), BF16),
            pltpu.VMEM((3 * NY, 8, BLK), jnp.int32),
            pltpu.VMEM((3 * ROW, BLK), F32),
            pltpu.VMEM((3 * ROW, HD), BF16),
            pltpu.VMEM((3 * ROW, HD), BF16),
            pltpu.VMEM((HD, WIN), BF16),
            pltpu.VMEM((HD, WIN), BF16),
            pltpu.VMEM((WIN, HD), BF16),
            pltpu.VMEM((WIN, WIN), BF16),
            pltpu.VMEM((WIN, WIN), BF16),
            pltpu.VMEM((STEPS, HD), F32),
            pltpu.VMEM((NZ, CLIPS, HD), F32),
            pltpu.VMEM((NZ, CLIPS, HD), F32),
            pltpu.VMEM((NZ, CLIPS, HD), F32),
            pltpu.VMEM((CLIPS, HD), F32),
            dma((5,)), dma((SLOTS,)), dma((SLOTS,)),
            dma((SLOTS, NY - 1)), dma((SLOTS, NY - 1)),
            dma((SLOTS, NY)), dma((SLOTS, NY)),
            dma((SLOTS, NY)), dma((SLOTS, NY)),
            dma((SLOTS, NY - 1)), dma((SLOTS, NY - 1)),
            dma((NY + 1,)), dma((NY + 1,)),
            dma((NZ - 1,)), dma((NZ - 1,)),
            dma((NZ,)), dma((NZ,)),
        ],
        compiler_params=pltpu.CompilerParams(
            collective_id=0, has_side_effects=True, vmem_limit_bytes=60 * 2**20
        ),
        cost_estimate=pl.CostEstimate(flops=12 * 2**30, bytes_accessed=8 * 2**20, transcendentals=2**23),
        name="clip_attention_backward",
    )(
        clip_step, clip_weight, queries, keys, values, cotangent,
        clip_ids.reshape(1, BLK), step_gate.reshape(STEPS, HD),
    )
    grads = jax.ShapeDtypeStruct((BLK, HEADS, HD), BF16)
    dq, dk, dv, table = pl.pallas_call(
        lay_out,
        out_shape=(grads, grads, grads, jax.ShapeDtypeStruct((STEPS, HD), F32)),
        in_specs=[sm, vm, hb],
        out_specs=(hb, hb, hb, hb),
        scratch_shapes=[
            pltpu.VMEM((3, 2, HEADS, BLK // 2, HD), BF16),
            pltpu.VMEM((3, 2, BLK // 2, HEADS, HD), BF16),
            pltpu.VMEM((STEPS, HD), F32),
            dma((3, 2)), dma((4, 2)),
        ],
        compiler_params=pltpu.CompilerParams(vmem_limit_bytes=60 * 2**20),
        cost_estimate=pl.CostEstimate(flops=2**25, bytes_accessed=7 * 2**20, transcendentals=0),
        name="lay_out",
    )(clip_step, total, fin)
    return dq, dk, dv, table.reshape(STEPS, 1, HD)


def solution(mesh):
    in_specs = (
        P(("dp", "seq"), None, None),
        P(("dp", "seq"), None, None),
        P(("dp", "seq"), None, None),
        P(("dp", "seq"), None, None),
        P(("dp", "seq")),
        P("dp"),
        P("dp"),
        P(None, "seq", None),
    )
    out_specs = (
        P(("dp", "seq"), None, None),
        P(("dp", "seq"), None, None),
        P(("dp", "seq"), None, None),
        P("dp", "seq", None),
    )
    return jax.shard_map(
        on_device, mesh=mesh, in_specs=in_specs, out_specs=out_specs, check_vma=False
    )
```

```python
import math

import jax
import jax.numpy as jnp
from jax import lax
from jax.experimental import pallas as pl
from jax.experimental.pallas import tpu as pltpu
from jax.sharding import PartitionSpec as P

NY = 4
NZ = 8
BLK = 128
ROW = NY * BLK
WIN = 2 * ROW
HD = 128
HEADS = 32
SLOTS = HEADS // NY
CLIPS = 16
STEPS = 1000
QB = 256
NEAR = 80.0
AHEAD = 2
FIRST = (0, 1, 2, 3, 5, 7)
LATER = ((4, 0), (6, 2))
LAG_COMPUTE = 3
LAG_BACK = 7
MESH = pl.DeviceIdType.MESH
F32 = jnp.float32
BF16 = jnp.bfloat16


def nt(a, b):
    return lax.dot_general(a, b, (((1,), (1,)), ((), ())), preferred_element_type=F32)


def nn(a, b):
    return jnp.dot(a, b, preferred_element_type=F32)


def fill_clips(idbuf, idcol, hot, near):
    lane = lax.broadcasted_iota(jnp.int32, (BLK, HD), 1)
    clip = (lane % CLIPS).astype(F32)
    once = jnp.where(lane < CLIPS, NEAR, 0.0)

    def one(b, _):
        at = pl.ds(pl.multiple_of(b * BLK, BLK), BLK)
        ids = jnp.broadcast_to(idbuf[b, 0:1, :].astype(F32), (BLK, BLK)).T
        idcol[at, :] = ids
        hot[at, :] = jnp.where(ids == clip, 1.0, 0.0).astype(BF16)
        near[at, :] = jnp.where(ids == clip, once, 0.0).astype(BF16)
        return 0

    lax.fori_loop(0, 3 * NY, one, 0)


def three_parts(x):
    hi = x.astype(BF16)
    rest = x - hi.astype(F32)
    mid = rest.astype(BF16)
    low = (rest - mid.astype(F32)).astype(BF16)
    return jnp.concatenate([hi, mid, low, jnp.zeros((HD - 3 * CLIPS, HD), BF16)], axis=0)


def other_clip(idcol, parity):
    return idcol[pl.ds(2 * ROW - (ROW + 1) * (1 - parity), 1), :]


def attend(i, win, res, gate_in, idbuf, idcol, hot, near, kt, vt, dout, probs, dscores):
    parity = lax.rem(i, 2)
    base = NY * (1 - parity)
    start = pl.multiple_of(base * BLK, BLK)
    kt[...] = win[i, 1].T
    vt[...] = win[i, 2].T
    scale = nn(hot[pl.ds(start, WIN), :], three_parts(gate_in[i]))
    dout[...] = (scale * win[i, 3].astype(F32)).astype(BF16)

    factor = 1.0 / math.sqrt(HD)
    per = QB // BLK
    not_mine = jnp.concatenate([other_clip(idcol, parity)] * per, axis=1)
    edge = jnp.concatenate([idcol[pl.ds(2 * ROW - ROW * parity - (1 - parity), 1), :]] * per, axis=1)
    cid = lax.broadcasted_iota(jnp.int32, (CLIPS, QB), 0).astype(F32)
    sums = jnp.zeros((CLIPS, HD), F32)
    for j in range(WIN // QB):
        lo, hi = max(0, j * QB - ROW), min(WIN, (j + 1) * QB + ROW)
        at = slice(j * QB, (j + 1) * QB)
        qb = win[i, 0, at, :]
        ids_q = jnp.concatenate([idbuf[base + j * per + u, 0:1, :] for u in range(per)], axis=1)
        ids_q = ids_q.astype(F32)
        near_k = near[pl.ds(pl.multiple_of(start + lo, QB), hi - lo), :]
        near_q = near[pl.ds(pl.multiple_of(start + j * QB, QB), QB), :]
        s = nt(jnp.concatenate([win[i, 1, lo:hi], near_k], axis=1), jnp.concatenate([qb, near_q], axis=1))
        top = jnp.max(s, axis=0, keepdims=True)
        e = jnp.exp2((s - top) * (factor * math.log2(math.e)))
        inv = 1.0 / jnp.sum(e, axis=0, keepdims=True)
        eb = e.astype(BF16)
        o = (nn(vt[:, lo:hi], eb) * inv).T.astype(BF16).astype(F32)
        db = (dout[at, :].astype(F32) * jnp.broadcast_to(inv, (HD, QB)).T).astype(BF16)
        dp = nt(win[i, 2, lo:hi], db)
        delta = jnp.sum((db.astype(F32) * o).T, axis=0, keepdims=True)
        ds = (e * (dp - delta)).astype(BF16)
        res[i, 0, at, :] = (nn(kt[:, lo:hi], ds) * factor).T.astype(BF16)
        probs[lo:hi, at] = eb
        dscores[lo:hi, at] = ds
        dout[at, :] = db
        halo = (j * QB // ROW + parity) % 2
        inside = jnp.full((1, QB), 1 - halo, jnp.int32).astype(F32)
        good = jnp.where(ids_q != not_mine, jnp.where(ids_q == edge, 1.0, inside), 0.0)
        pick = jnp.where(cid == ids_q, good, 0.0).astype(BF16)
        prod = win[i, 3, at, :].astype(F32) * o
        ph = prod.astype(BF16)
        sums = sums + (nn(pick, ph) + nn(pick, (prod - ph.astype(F32)).astype(BF16)))
    for k0, k1 in ((0, QB), (QB, WIN - QB), (WIN - QB, WIN)):
        q0, q1 = max(0, k0 - ROW), min(WIN, k1 + ROW)
        res[i, 1, k0:k1] = (nn(dscores[k0:k1, q0:q1], win[i, 0, q0:q1]) * factor).astype(BF16)
        res[i, 2, k0:k1] = nn(probs[k0:k1, q0:q1], dout[q0:q1]).astype(BF16)
    return sums


def kernel(
    step_ref, weight_ref, q_hbm, k_hbm, v_hbm, c_hbm, ids_ref, gate_hbm,
    fin_hbm, total_ref,
    stage, src, win, res, back, idbuf, idcol, hot, near, kt, vt, dout, probs, dscores,
    gates, gate_in, sum_in, sum_out, wcol,
    load_sem, own_sem, fin_sem,
    yin_s, yin_r, zin_s, zin_r, zout_s, zout_r, yout_s, yout_r, id_s, id_r, gate_s, gate_r, sum_s, sum_r,
):
    me = lax.axis_index("seq")
    z, y = me // NY, lax.rem(me, NY)

    def ypeer(d):
        return {"seq": z * NY + lax.rem(y + d, NY)}

    def zpeer(d):
        return {"seq": lax.rem(z + d, NZ) * NY + y}

    gate_load = pltpu.make_async_copy(gate_hbm, gates, load_sem.at[4])
    loads = [
        pltpu.make_async_copy(r, stage.at[a], load_sem.at[a])
        for a, r in enumerate((q_hbm, k_hbm, v_hbm, c_hbm))
    ]
    for c in loads:
        c.start()
    gate_load.start()

    barrier = pltpu.get_barrier_semaphore()
    for d in range(1, NY):
        pl.semaphore_signal(barrier, inc=1, device_id=ypeer(d), device_id_type=MESH)
    for d in range(1, NZ):
        pl.semaphore_signal(barrier, inc=1, device_id=zpeer(d), device_id_type=MESH)

    idbuf[NY + y] = jnp.broadcast_to(ids_ref[...], (8, BLK))
    for a, c in enumerate(loads):
        c.wait()
        src[:, a] = jnp.swapaxes(stage[a], 0, 1)

    def remote(s, d, ss, rs, to):
        return pltpu.make_async_remote_copy(
            src_ref=s, dst_ref=d, send_sem=ss, recv_sem=rs, device_id=to, device_id_type=MESH
        )

    def part(first, b):
        return pl.ds(pl.multiple_of(first + b * BLK, BLK), BLK)

    def own_at(i):
        return ROW * lax.rem(i, 2)

    def yin(i, d):
        return remote(
            src.at[NY * i + lax.rem(y + d, NY)], win.at[i, :, part(own_at(i), y), :],
            yin_s.at[i, d - 1], yin_r.at[i, d - 1], ypeer(d),
        )

    def own_copy(i):
        return pltpu.make_async_copy(
            src.at[NY * i + y], win.at[i, :, part(own_at(i), y), :], own_sem.at[i]
        )

    def zin_to(i):
        return zpeer(jnp.where(lax.rem(i, 2) == 0, NZ - 1, 1))

    def zin(i, b):
        return remote(
            win.at[i, :, part(own_at(i), b), :], win.at[i, :, part(ROW - own_at(i), b), :],
            zin_s.at[i, b], zin_r.at[i, b], zin_to(i),
        )

    def zin_own(i):
        return remote(
            src.at[NY * i + y], win.at[i, :, part(ROW - own_at(i), y), :],
            zin_s.at[i, y], zin_r.at[i, y], zin_to(i),
        )

    def zout(i, b):
        return remote(
            res.at[i, :, part(ROW - own_at(i), b), :], back.at[i, :, part(0, b), :],
            zout_s.at[i, b], zout_r.at[i, b], zpeer(jnp.where(lax.rem(i, 2) == 0, 1, NZ - 1)),
        )

    def yout(i, d):
        return remote(
            res.at[i, :, part(own_at(i), lax.rem(y + d, NY)), :], fin_hbm.at[NY * i + y],
            yout_s.at[i, d - 1], yout_r.at[i, d - 1], ypeer(d),
        )

    def fin_own(i):
        return pltpu.make_async_copy(
            res.at[i, :, part(own_at(i), y), :], fin_hbm.at[NY * i + y], fin_sem.at[i]
        )

    def id_y(d):
        return remote(idbuf.at[NY + y], idbuf.at[NY + y], id_s.at[d - 1], id_r.at[d - 1], ypeer(d))

    def id_z(n):
        return remote(
            idbuf.at[pl.ds(NY, NY)], idbuf.at[pl.ds(2 * NY * n, NY)],
            id_s.at[NY - 1 + n], id_r.at[NY - 1 + n], zpeer(1 if n == 0 else NZ - 1),
        )

    def gate_copy(d):
        return remote(gate_in.at[z], gate_in.at[z], gate_s.at[d - 1], gate_r.at[d - 1], zpeer(d))

    def sum_copy(i, slot):
        return remote(
            sum_out.at[i], sum_in.at[slot], sum_s.at[i], sum_r.at[slot], zpeer(lax.rem(i - z + NZ, NZ))
        )

    def begin(i):
        for d in range(1, NY):
            yin(i, d).start()
        own_copy(i).start()

    pl.semaphore_wait(barrier, NY - 1 + NZ - 1)
    for d in range(1, NY):
        id_y(d).start()
    begin(jnp.int32(0))

    for i in FIRST:
        zin_own(jnp.int32(i)).start()
    for i in range(1, AHEAD):
        begin(jnp.int32(i))
    gate_load.wait()
    for c in range(CLIPS):
        wcol[c : c + 1, :] = jnp.full((1, HD), weight_ref[c], F32)
        gate_in[z, c : c + 1, :] = gates[pl.ds(step_ref[c], 1), :] * weight_ref[c]
    for d in range(1, NZ):
        gate_copy(d).start()
    for d in range(1, NY):
        id_y(d).wait_recv()
    for n in range(2):
        id_z(n).start()

    def step(t, _):
        @pl.when(t < SLOTS)
        def _():
            for d in range(1, NY):
                yin(t, d).wait_recv()
                zin(t, lax.rem(y + NY - d, NY)).start()
            own_copy(t).wait()
            for i, after in LATER:

                @pl.when(t == after)
                def _():
                    zin_own(jnp.int32(i)).start()

            @pl.when(t + AHEAD < SLOTS)
            def _():
                begin(t + AHEAD)

        @pl.when(t == 1)
        def _():
            for n in range(2):
                id_z(n).wait_recv()
            fill_clips(idbuf, idcol, hot, near)
            for d in range(1, NZ):
                gate_copy(d).wait_recv()

        @pl.when((t >= LAG_COMPUTE) & (t < SLOTS + LAG_COMPUTE))
        def _():
            i = t - LAG_COMPUTE
            for b in range(NY):
                zin(i, b).wait_recv()
            sums = attend(
                i, win, res, gate_in, idbuf, idcol, hot, near, kt, vt, dout, probs, dscores
            )
            for d in (1, 2, 3, 0):
                zout(i, lax.rem(y + d, NY)).start()
            sum_out[i] = sums * wcol[...]

            @pl.when(i != z)
            def _():
                sum_copy(i, z).start()

            @pl.when(i == z)
            def _():
                sum_in[z] = sum_out[i]

        @pl.when((t >= LAG_BACK) & (t != LAG_BACK + 2))
        def _():
            for d in (1, 2, 3, 0):
                b = lax.rem(y + d, NY)
                for odd in range(2):
                    i = 2 * (t - LAG_BACK - jnp.where(t > LAG_BACK + 2, 1, 0)) + odd
                    zout(i, b).wait_recv()
                    theirs = idcol[part(ROW, b), :] == other_clip(idcol, odd)
                    for a in range(3):
                        res[i, a, part(ROW * odd, b), :] = jnp.where(
                            theirs,
                            back[i, a, part(0, b), :].astype(F32),
                            res[i, a, part(ROW * odd, b), :].astype(F32),
                        ).astype(BF16)
                    if d:
                        yout(i, d).start()
                    else:
                        fin_own(i).start()

        return 0

    lax.fori_loop(0, LAG_BACK + SLOTS // 2 + 1, step, 0)

    def sums_arrived(i, _):
        @pl.when(i != z)
        def _():
            sum_copy(i, i).wait_recv()

        return 0

    lax.fori_loop(0, NZ, sums_arrived, 0)
    total = sum_in[0]
    for r in range(1, NZ):
        total = total + sum_in[r]
    total_ref[...] = total

    def done(i, _):
        for d in range(1, NY):
            yin(i, d).wait_send()
            yout(i, d).wait_send()
            yout(i, d).wait_recv()
        for b in range(NY):
            zin(i, b).wait_send()
            zout(i, b).wait_send()
        fin_own(i).wait()

        @pl.when(i != z)
        def _():
            sum_copy(i, z).wait_send()

        return 0

    lax.fori_loop(0, SLOTS, done, 0)
    for d in range(1, NY):
        id_y(d).wait_send()
    for n in range(2):
        id_z(n).wait_send()
    for d in range(1, NZ):
        gate_copy(d).wait_send()


def lay_out(step_ref, total_ref, fin_hbm, dq_hbm, dk_hbm, dv_hbm, table_hbm, got, put, table, in_sem, out_sem):
    half = BLK // 2
    pieces = [(a, n) for a in range(3) for n in range(2)]
    ins = [
        pltpu.make_async_copy(
            fin_hbm.at[:, a, n * half : (n + 1) * half, :], got.at[a, n], in_sem.at[a, n]
        )
        for a, n in pieces
    ]
    outs = [
        pltpu.make_async_copy(
            put.at[a, n], (dq_hbm, dk_hbm, dv_hbm)[a].at[n * half : (n + 1) * half], out_sem.at[a, n]
        )
        for a, n in pieces
    ]
    for c in ins:
        c.start()
    lane = lax.broadcasted_iota(jnp.int32, (1, HD), 1) % CLIPS
    steps = jnp.zeros((1, HD), jnp.int32)
    for c in range(CLIPS):
        steps = jnp.where(lane == c, step_ref[c], steps)
    line = lax.broadcasted_iota(jnp.int32, (STEPS, HD), 0)
    pick = jnp.where(line == steps, 1.0, 0.0).astype(BF16)
    table[...] = nn(pick, three_parts(total_ref[...]))
    table_out = pltpu.make_async_copy(table, table_hbm, out_sem.at[3, 0])
    table_out.start()
    for (a, n), i, o in zip(pieces, ins, outs):
        i.wait()
        put[a, n] = jnp.swapaxes(got[a, n], 0, 1)
        o.start()
    for o in outs:
        o.wait()
    table_out.wait()


def on_device(queries, keys, values, cotangent, clip_ids, clip_step, clip_weight, step_gate):
    vm = pl.BlockSpec(memory_space=pltpu.VMEM)
    sm = pl.BlockSpec(memory_space=pltpu.SMEM)
    hb = pl.BlockSpec(memory_space=pl.ANY)
    dma = pltpu.SemaphoreType.DMA
    fin, total = pl.pallas_call(
        kernel,
        out_shape=(
            jax.ShapeDtypeStruct((HEADS, 3, BLK, HD), BF16),
            jax.ShapeDtypeStruct((CLIPS, HD), F32),
        ),
        in_specs=[sm, sm, hb, hb, hb, hb, vm, hb],
        out_specs=(hb, vm),
        scratch_shapes=[
            pltpu.VMEM((4, BLK, HEADS, HD), BF16),
            pltpu.VMEM((HEADS, 4, BLK, HD), BF16),
            pltpu.VMEM((SLOTS, 4, WIN, HD), BF16),
            pltpu.VMEM((SLOTS, 3, WIN, HD), BF16),
            pltpu.VMEM((SLOTS, 3, ROW, HD), BF16),
            pltpu.VMEM((3 * NY, 8, BLK), jnp.int32),
            pltpu.VMEM((3 * ROW, BLK), F32),
            pltpu.VMEM((3 * ROW, HD), BF16),
            pltpu.VMEM((3 * ROW, HD), BF16),
            pltpu.VMEM((HD, WIN), BF16),
            pltpu.VMEM((HD, WIN), BF16),
            pltpu.VMEM((WIN, HD), BF16),
            pltpu.VMEM((WIN, WIN), BF16),
            pltpu.VMEM((WIN, WIN), BF16),
            pltpu.VMEM((STEPS, HD), F32),
            pltpu.VMEM((NZ, CLIPS, HD), F32),
            pltpu.VMEM((NZ, CLIPS, HD), F32),
            pltpu.VMEM((NZ, CLIPS, HD), F32),
            pltpu.VMEM((CLIPS, HD), F32),
            dma((5,)), dma((SLOTS,)), dma((SLOTS,)),
            dma((SLOTS, NY - 1)), dma((SLOTS, NY - 1)),
            dma((SLOTS, NY)), dma((SLOTS, NY)),
            dma((SLOTS, NY)), dma((SLOTS, NY)),
            dma((SLOTS, NY - 1)), dma((SLOTS, NY - 1)),
            dma((NY + 1,)), dma((NY + 1,)),
            dma((NZ - 1,)), dma((NZ - 1,)),
            dma((NZ,)), dma((NZ,)),
        ],
        compiler_params=pltpu.CompilerParams(
            collective_id=0, has_side_effects=True, vmem_limit_bytes=60 * 2**20
        ),
        cost_estimate=pl.CostEstimate(flops=12 * 2**30, bytes_accessed=8 * 2**20, transcendentals=2**23),
        name="clip_attention_backward",
    )(
        clip_step, clip_weight, queries, keys, values, cotangent,
        clip_ids.reshape(1, BLK), step_gate.reshape(STEPS, HD),
    )
    grads = jax.ShapeDtypeStruct((BLK, HEADS, HD), BF16)
    dq, dk, dv, table = pl.pallas_call(
        lay_out,
        out_shape=(grads, grads, grads, jax.ShapeDtypeStruct((STEPS, HD), F32)),
        in_specs=[sm, vm, hb],
        out_specs=(hb, hb, hb, hb),
        scratch_shapes=[
            pltpu.VMEM((3, 2, HEADS, BLK // 2, HD), BF16),
            pltpu.VMEM((3, 2, BLK // 2, HEADS, HD), BF16),
            pltpu.VMEM((STEPS, HD), F32),
            dma((3, 2)), dma((4, 2)),
        ],
        compiler_params=pltpu.CompilerParams(vmem_limit_bytes=60 * 2**20),
        cost_estimate=pl.CostEstimate(flops=2**25, bytes_accessed=7 * 2**20, transcendentals=0),
        name="lay_out",
    )(clip_step, total, fin)
    return dq, dk, dv, table.reshape(STEPS, 1, HD)


def solution(mesh):
    in_specs = (
        P(("dp", "seq"), None, None),
        P(("dp", "seq"), None, None),
        P(("dp", "seq"), None, None),
        P(("dp", "seq"), None, None),
        P(("dp", "seq")),
        P("dp"),
        P("dp"),
        P(None, "seq", None),
    )
    out_specs = (
        P(("dp", "seq"), None, None),
        P(("dp", "seq"), None, None),
        P(("dp", "seq"), None, None),
        P("dp", "seq", None),
    )
    return jax.shard_map(
        on_device, mesh=mesh, in_specs=in_specs, out_specs=out_specs, check_vma=False
    )
```

```python
import math

import jax
import jax.numpy as jnp
from jax import lax
from jax.experimental import pallas as pl
from jax.experimental.pallas import tpu as pltpu
from jax.sharding import PartitionSpec as P

NY = 4
NZ = 8
BLK = 128
ROW = NY * BLK
WIN = 2 * ROW
HD = 128
HEADS = 32
SLOTS = HEADS // NY
CLIPS = 16
STEPS = 1000
QB = 256
NEAR = 80.0
AHEAD = 2
FIRST = (0, 1, 2, 3, 5, 7)
LATER = ((4, 0), (6, 2))
LAG_COMPUTE = 3
LAG_BACK = 6
MESH = pl.DeviceIdType.MESH
F32 = jnp.float32
BF16 = jnp.bfloat16


def nt(a, b):
    return lax.dot_general(a, b, (((1,), (1,)), ((), ())), preferred_element_type=F32)


def nn(a, b):
    return jnp.dot(a, b, preferred_element_type=F32)


def fill_clips(idbuf, idcol, hot, near):
    lane = lax.broadcasted_iota(jnp.int32, (BLK, HD), 1)
    clip = (lane % CLIPS).astype(F32)
    once = jnp.where(lane < CLIPS, NEAR, 0.0)

    def one(b, _):
        at = pl.ds(pl.multiple_of(b * BLK, BLK), BLK)
        ids = jnp.broadcast_to(idbuf[b, 0:1, :].astype(F32), (BLK, BLK)).T
        idcol[at, :] = ids
        hot[at, :] = jnp.where(ids == clip, 1.0, 0.0).astype(BF16)
        near[at, :] = jnp.where(ids == clip, once, 0.0).astype(BF16)
        return 0

    lax.fori_loop(0, 3 * NY, one, 0)


def three_parts(x):
    hi = x.astype(BF16)
    rest = x - hi.astype(F32)
    mid = rest.astype(BF16)
    low = (rest - mid.astype(F32)).astype(BF16)
    return jnp.concatenate([hi, mid, low, jnp.zeros((HD - 3 * CLIPS, HD), BF16)], axis=0)


def other_clip(idcol, parity):
    return idcol[pl.ds(2 * ROW - (ROW + 1) * (1 - parity), 1), :]


def attend(i, win, res, gate_in, idbuf, idcol, hot, near, kt, vt, dout, probs, dscores):
    parity = lax.rem(i, 2)
    base = NY * (1 - parity)
    start = pl.multiple_of(base * BLK, BLK)
    kt[...] = win[i, 1].T
    vt[...] = win[i, 2].T
    scale = nn(hot[pl.ds(start, WIN), :], three_parts(gate_in[i]))
    dout[...] = (scale * win[i, 3].astype(F32)).astype(BF16)

    factor = 1.0 / math.sqrt(HD)
    per = QB // BLK
    not_mine = jnp.concatenate([other_clip(idcol, parity)] * per, axis=1)
    edge = jnp.concatenate([idcol[pl.ds(2 * ROW - ROW * parity - (1 - parity), 1), :]] * per, axis=1)
    cid = lax.broadcasted_iota(jnp.int32, (CLIPS, QB), 0).astype(F32)
    sums = jnp.zeros((CLIPS, HD), F32)
    for j in range(WIN // QB):
        lo, hi = max(0, j * QB - ROW), min(WIN, (j + 1) * QB + ROW)
        at = slice(j * QB, (j + 1) * QB)
        qb = win[i, 0, at, :]
        ids_q = jnp.concatenate([idbuf[base + j * per + u, 0:1, :] for u in range(per)], axis=1)
        ids_q = ids_q.astype(F32)
        near_k = near[pl.ds(pl.multiple_of(start + lo, QB), hi - lo), :]
        near_q = near[pl.ds(pl.multiple_of(start + j * QB, QB), QB), :]
        s = nt(jnp.concatenate([win[i, 1, lo:hi], near_k], axis=1), jnp.concatenate([qb, near_q], axis=1))
        top = jnp.max(s, axis=0, keepdims=True)
        e = jnp.exp2((s - top) * (factor * math.log2(math.e)))
        inv = 1.0 / jnp.sum(e, axis=0, keepdims=True)
        eb = e.astype(BF16)
        o = (nn(vt[:, lo:hi], eb) * inv).T.astype(BF16).astype(F32)
        db = (dout[at, :].astype(F32) * jnp.broadcast_to(inv, (HD, QB)).T).astype(BF16)
        dp = nt(win[i, 2, lo:hi], db)
        delta = jnp.sum((db.astype(F32) * o).T, axis=0, keepdims=True)
        ds = (e * (dp - delta)).astype(BF16)
        res[i, 0, at, :] = (nn(kt[:, lo:hi], ds) * factor).T.astype(BF16)
        probs[lo:hi, at] = eb
        dscores[lo:hi, at] = ds
        dout[at, :] = db
        halo = (j * QB // ROW + parity) % 2
        inside = jnp.full((1, QB), 1 - halo, jnp.int32).astype(F32)
        good = jnp.where(ids_q != not_mine, jnp.where(ids_q == edge, 1.0, inside), 0.0)
        pick = jnp.where(cid == ids_q, good, 0.0).astype(BF16)
        prod = win[i, 3, at, :].astype(F32) * o
        ph = prod.astype(BF16)
        sums = sums + (nn(pick, ph) + nn(pick, (prod - ph.astype(F32)).astype(BF16)))
    for k0, k1 in ((0, QB), (QB, WIN - QB), (WIN - QB, WIN)):
        q0, q1 = max(0, k0 - ROW), min(WIN, k1 + ROW)
        res[i, 1, k0:k1] = (nn(dscores[k0:k1, q0:q1], win[i, 0, q0:q1]) * factor).astype(BF16)
        res[i, 2, k0:k1] = nn(probs[k0:k1, q0:q1], dout[q0:q1]).astype(BF16)
    return sums


def kernel(
    step_ref, weight_ref, q_hbm, k_hbm, v_hbm, c_hbm, ids_ref, gate_hbm,
    fin_hbm, total_ref,
    stage, src, win, res, back, idbuf, idcol, hot, near, kt, vt, dout, probs, dscores,
    gates, gate_in, sum_in, sum_out, wcol,
    load_sem, own_sem, fin_sem,
    yin_s, yin_r, zin_s, zin_r, zout_s, zout_r, yout_s, yout_r, id_s, id_r, gate_s, gate_r, sum_s, sum_r,
):
    me = lax.axis_index("seq")
    z, y = me // NY, lax.rem(me, NY)

    def ypeer(d):
        return {"seq": z * NY + lax.rem(y + d, NY)}

    def zpeer(d):
        return {"seq": lax.rem(z + d, NZ) * NY + y}

    gate_load = pltpu.make_async_copy(gate_hbm, gates, load_sem.at[4])
    loads = [
        pltpu.make_async_copy(r, stage.at[a], load_sem.at[a])
        for a, r in enumerate((q_hbm, k_hbm, v_hbm, c_hbm))
    ]
    for c in loads:
        c.start()
    gate_load.start()

    barrier = pltpu.get_barrier_semaphore()
    for d in range(1, NY):
        pl.semaphore_signal(barrier, inc=1, device_id=ypeer(d), device_id_type=MESH)
    for d in range(1, NZ):
        pl.semaphore_signal(barrier, inc=1, device_id=zpeer(d), device_id_type=MESH)

    idbuf[NY + y] = jnp.broadcast_to(ids_ref[...], (8, BLK))
    for a, c in enumerate(loads):
        c.wait()
        src[:, a] = jnp.swapaxes(stage[a], 0, 1)

    def remote(s, d, ss, rs, to):
        return pltpu.make_async_remote_copy(
            src_ref=s, dst_ref=d, send_sem=ss, recv_sem=rs, device_id=to, device_id_type=MESH
        )

    def part(first, b):
        return pl.ds(pl.multiple_of(first + b * BLK, BLK), BLK)

    def own_at(i):
        return ROW * lax.rem(i, 2)

    def yin(i, d):
        return remote(
            src.at[NY * i + lax.rem(y + d, NY)], win.at[i, :, part(own_at(i), y), :],
            yin_s.at[i, d - 1], yin_r.at[i, d - 1], ypeer(d),
        )

    def own_copy(i):
        return pltpu.make_async_copy(
            src.at[NY * i + y], win.at[i, :, part(own_at(i), y), :], own_sem.at[i]
        )

    def zin_to(i):
        return zpeer(jnp.where(lax.rem(i, 2) == 0, NZ - 1, 1))

    def zin(i, b):
        return remote(
            win.at[i, :, part(own_at(i), b), :], win.at[i, :, part(ROW - own_at(i), b), :],
            zin_s.at[i, b], zin_r.at[i, b], zin_to(i),
        )

    def zin_own(i):
        return remote(
            src.at[NY * i + y], win.at[i, :, part(ROW - own_at(i), y), :],
            zin_s.at[i, y], zin_r.at[i, y], zin_to(i),
        )

    def zout(i, b):
        return remote(
            res.at[i, :, part(ROW - own_at(i), b), :], back.at[i, :, part(0, b), :],
            zout_s.at[i, b], zout_r.at[i, b], zpeer(jnp.where(lax.rem(i, 2) == 0, 1, NZ - 1)),
        )

    def yout(i, d):
        return remote(
            res.at[i, :, part(own_at(i), lax.rem(y + d, NY)), :], fin_hbm.at[NY * i + y],
            yout_s.at[i, d - 1], yout_r.at[i, d - 1], ypeer(d),
        )

    def fin_own(i):
        return pltpu.make_async_copy(
            res.at[i, :, part(own_at(i), y), :], fin_hbm.at[NY * i + y], fin_sem.at[i]
        )

    def id_y(d):
        return remote(idbuf.at[NY + y], idbuf.at[NY + y], id_s.at[d - 1], id_r.at[d - 1], ypeer(d))

    def id_z(n):
        return remote(
            idbuf.at[pl.ds(NY, NY)], idbuf.at[pl.ds(2 * NY * n, NY)],
            id_s.at[NY - 1 + n], id_r.at[NY - 1 + n], zpeer(1 if n == 0 else NZ - 1),
        )

    def gate_copy(d):
        return remote(gate_in.at[z], gate_in.at[z], gate_s.at[d - 1], gate_r.at[d - 1], zpeer(d))

    def sum_copy(i, slot):
        return remote(
            sum_out.at[i], sum_in.at[slot], sum_s.at[i], sum_r.at[slot], zpeer(lax.rem(i - z + NZ, NZ))
        )

    def begin(i):
        for d in range(1, NY):
            yin(i, d).start()
        own_copy(i).start()

    pl.semaphore_wait(barrier, NY - 1 + NZ - 1)
    for d in range(1, NY):
        id_y(d).start()
    begin(jnp.int32(0))

    for i in FIRST:
        zin_own(jnp.int32(i)).start()
    for i in range(1, AHEAD):
        begin(jnp.int32(i))
    gate_load.wait()
    for c in range(CLIPS):
        wcol[c : c + 1, :] = jnp.full((1, HD), weight_ref[c], F32)
        gate_in[z, c : c + 1, :] = gates[pl.ds(step_ref[c], 1), :] * weight_ref[c]
    for d in range(1, NZ):
        gate_copy(d).start()
    for d in range(1, NY):
        id_y(d).wait_recv()
    for n in range(2):
        id_z(n).start()

    def step(t, _):
        @pl.when(t < SLOTS)
        def _():
            for d in range(1, NY):
                yin(t, d).wait_recv()
                zin(t, lax.rem(y + NY - d, NY)).start()
            own_copy(t).wait()
            for i, after in LATER:

                @pl.when(t == after)
                def _():
                    zin_own(jnp.int32(i)).start()

            @pl.when(t + AHEAD < SLOTS)
            def _():
                begin(t + AHEAD)

        @pl.when(t == 1)
        def _():
            for n in range(2):
                id_z(n).wait_recv()
            fill_clips(idbuf, idcol, hot, near)
            for d in range(1, NZ):
                gate_copy(d).wait_recv()

        @pl.when((t >= LAG_COMPUTE) & (t < SLOTS + LAG_COMPUTE))
        def _():
            i = t - LAG_COMPUTE
            for b in range(NY):
                zin(i, b).wait_recv()
            sums = attend(
                i, win, res, gate_in, idbuf, idcol, hot, near, kt, vt, dout, probs, dscores
            )
            for d in (1, 2, 3, 0):
                zout(i, lax.rem(y + d, NY)).start()
            sum_out[i] = sums * wcol[...]

            @pl.when(i != z)
            def _():
                sum_copy(i, z).start()

            @pl.when(i == z)
            def _():
                sum_in[z] = sum_out[i]

        def take_back(i, d):
            b = lax.rem(y + d, NY)
            zout(i, b).wait_recv()
            theirs = idcol[part(ROW, b), :] == other_clip(idcol, lax.rem(i, 2))
            for a in range(3):
                res[i, a, part(own_at(i), b), :] = jnp.where(
                    theirs,
                    back[i, a, part(0, b), :].astype(F32),
                    res[i, a, part(own_at(i), b), :].astype(F32),
                ).astype(BF16)
            if d:
                yout(i, d).start()
            else:
                fin_own(i).start()

        @pl.when((t >= LAG_BACK) & (t < LAG_BACK + SLOTS // 2))
        def _():
            for d in (1, 2, 3, 0):
                take_back(t - LAG_BACK, d)

        @pl.when(t >= LAG_BACK + SLOTS // 2)
        def _():
            for d in (1, 2, 3, 0):
                for odd in range(2):
                    take_back(2 * (t - LAG_BACK) - SLOTS // 2 + odd, d)

        return 0

    lax.fori_loop(0, LAG_BACK + SLOTS * 3 // 4, step, 0)

    def sums_arrived(i, _):
        @pl.when(i != z)
        def _():
            sum_copy(i, i).wait_recv()

        return 0

    lax.fori_loop(0, NZ, sums_arrived, 0)
    total = sum_in[0]
    for r in range(1, NZ):
        total = total + sum_in[r]
    total_ref[...] = total

    def done(i, _):
        for d in range(1, NY):
            yin(i, d).wait_send()
            yout(i, d).wait_send()
            yout(i, d).wait_recv()
        for b in range(NY):
            zin(i, b).wait_send()
            zout(i, b).wait_send()
        fin_own(i).wait()

        @pl.when(i != z)
        def _():
            sum_copy(i, z).wait_send()

        return 0

    lax.fori_loop(0, SLOTS, done, 0)
    for d in range(1, NY):
        id_y(d).wait_send()
    for n in range(2):
        id_z(n).wait_send()
    for d in range(1, NZ):
        gate_copy(d).wait_send()


def lay_out(step_ref, total_ref, fin_hbm, dq_hbm, dk_hbm, dv_hbm, table_hbm, got, put, table, in_sem, out_sem):
    half = BLK // 2
    pieces = [(a, n) for a in range(3) for n in range(2)]
    ins = [
        pltpu.make_async_copy(
            fin_hbm.at[:, a, n * half : (n + 1) * half, :], got.at[a, n], in_sem.at[a, n]
        )
        for a, n in pieces
    ]
    outs = [
        pltpu.make_async_copy(
            put.at[a, n], (dq_hbm, dk_hbm, dv_hbm)[a].at[n * half : (n + 1) * half], out_sem.at[a, n]
        )
        for a, n in pieces
    ]
    for c in ins:
        c.start()
    lane = lax.broadcasted_iota(jnp.int32, (1, HD), 1) % CLIPS
    steps = jnp.zeros((1, HD), jnp.int32)
    for c in range(CLIPS):
        steps = jnp.where(lane == c, step_ref[c], steps)
    line = lax.broadcasted_iota(jnp.int32, (STEPS, HD), 0)
    pick = jnp.where(line == steps, 1.0, 0.0).astype(BF16)
    table[...] = nn(pick, three_parts(total_ref[...]))
    table_out = pltpu.make_async_copy(table, table_hbm, out_sem.at[3, 0])
    table_out.start()
    for (a, n), i, o in zip(pieces, ins, outs):
        i.wait()
        put[a, n] = jnp.swapaxes(got[a, n], 0, 1)
        o.start()
    for o in outs:
        o.wait()
    table_out.wait()


def on_device(queries, keys, values, cotangent, clip_ids, clip_step, clip_weight, step_gate):
    vm = pl.BlockSpec(memory_space=pltpu.VMEM)
    sm = pl.BlockSpec(memory_space=pltpu.SMEM)
    hb = pl.BlockSpec(memory_space=pl.ANY)
    dma = pltpu.SemaphoreType.DMA
    fin, total = pl.pallas_call(
        kernel,
        out_shape=(
            jax.ShapeDtypeStruct((HEADS, 3, BLK, HD), BF16),
            jax.ShapeDtypeStruct((CLIPS, HD), F32),
        ),
        in_specs=[sm, sm, hb, hb, hb, hb, vm, hb],
        out_specs=(hb, vm),
        scratch_shapes=[
            pltpu.VMEM((4, BLK, HEADS, HD), BF16),
            pltpu.VMEM((HEADS, 4, BLK, HD), BF16),
            pltpu.VMEM((SLOTS, 4, WIN, HD), BF16),
            pltpu.VMEM((SLOTS, 3, WIN, HD), BF16),
            pltpu.VMEM((SLOTS, 3, ROW, HD), BF16),
            pltpu.VMEM((3 * NY, 8, BLK), jnp.int32),
            pltpu.VMEM((3 * ROW, BLK), F32),
            pltpu.VMEM((3 * ROW, HD), BF16),
            pltpu.VMEM((3 * ROW, HD), BF16),
            pltpu.VMEM((HD, WIN), BF16),
            pltpu.VMEM((HD, WIN), BF16),
            pltpu.VMEM((WIN, HD), BF16),
            pltpu.VMEM((WIN, WIN), BF16),
            pltpu.VMEM((WIN, WIN), BF16),
            pltpu.VMEM((STEPS, HD), F32),
            pltpu.VMEM((NZ, CLIPS, HD), F32),
            pltpu.VMEM((NZ, CLIPS, HD), F32),
            pltpu.VMEM((NZ, CLIPS, HD), F32),
            pltpu.VMEM((CLIPS, HD), F32),
            dma((5,)), dma((SLOTS,)), dma((SLOTS,)),
            dma((SLOTS, NY - 1)), dma((SLOTS, NY - 1)),
            dma((SLOTS, NY)), dma((SLOTS, NY)),
            dma((SLOTS, NY)), dma((SLOTS, NY)),
            dma((SLOTS, NY - 1)), dma((SLOTS, NY - 1)),
            dma((NY + 1,)), dma((NY + 1,)),
            dma((NZ - 1,)), dma((NZ - 1,)),
            dma((NZ,)), dma((NZ,)),
        ],
        compiler_params=pltpu.CompilerParams(
            collective_id=0, has_side_effects=True, vmem_limit_bytes=60 * 2**20
        ),
        cost_estimate=pl.CostEstimate(flops=12 * 2**30, bytes_accessed=8 * 2**20, transcendentals=2**23),
        name="clip_attention_backward",
    )(
        clip_step, clip_weight, queries, keys, values, cotangent,
        clip_ids.reshape(1, BLK), step_gate.reshape(STEPS, HD),
    )
    grads = jax.ShapeDtypeStruct((BLK, HEADS, HD), BF16)
    dq, dk, dv, table = pl.pallas_call(
        lay_out,
        out_shape=(grads, grads, grads, jax.ShapeDtypeStruct((STEPS, HD), F32)),
        in_specs=[sm, vm, hb],
        out_specs=(hb, hb, hb, hb),
        scratch_shapes=[
            pltpu.VMEM((3, 2, HEADS, BLK // 2, HD), BF16),
            pltpu.VMEM((3, 2, BLK // 2, HEADS, HD), BF16),
            pltpu.VMEM((STEPS, HD), F32),
            dma((3, 2)), dma((4, 2)),
        ],
        compiler_params=pltpu.CompilerParams(vmem_limit_bytes=60 * 2**20),
        cost_estimate=pl.CostEstimate(flops=2**25, bytes_accessed=7 * 2**20, transcendentals=0),
        name="lay_out",
    )(clip_step, total, fin)
    return dq, dk, dv, table.reshape(STEPS, 1, HD)


def solution(mesh):
    in_specs = (
        P(("dp", "seq"), None, None),
        P(("dp", "seq"), None, None),
        P(("dp", "seq"), None, None),
        P(("dp", "seq"), None, None),
        P(("dp", "seq")),
        P("dp"),
        P("dp"),
        P(None, "seq", None),
    )
    out_specs = (
        P(("dp", "seq"), None, None),
        P(("dp", "seq"), None, None),
        P(("dp", "seq"), None, None),
        P("dp", "seq", None),
    )
    return jax.shard_map(
        on_device, mesh=mesh, in_specs=in_specs, out_specs=out_specs, check_vma=False
    )
```
